128 devices in a mesh: gx: 16 (over z, y), gy: 8 (over x, core).
Axes of the slice: x: 4, y: 4, z: 4, core: 2. Of those that a mesh axis runs over, the one named last changes fastest.
Arguments:
- inputs: bfloat16 [2, 64, 64, 64, 512], P(None, 'gx', 'gy'), may hold values from -6 to 6
- cotangent: bfloat16 [2, 64, 64, 64, 512], P(None, 'gx', 'gy'), may hold values from -6 to 6
- pre_activation: bfloat16 [2, 64, 64, 64, 512], P(None, 'gx', 'gy'), may hold values from -6 to 6
- pointwise: bfloat16 [32, 32], replicated, may hold values from -1 to 1
- spectral: bfloat16 [24, 24, 192, 1024], P(None, 'gy', 'gx'), may hold values from -4 to 4
Outputs:
- input_grad: bfloat16 [2, 64, 64, 64, 512], P(None, 'gx', 'gy')
- spectral_grad: float32 [24, 24, 192, 1024], P(None, 'gy', 'gx')
The draws below stay inside these ranges and needn't reach their ends.
All inputs are finite; a program needn't handle non-finite values.
Results may differ from the reference program's by a relative error of at most 0.0083.
Values sent between devices are 32-bit elements; how exact they have to be, the bound alone decides.
No kernel may reach another device: no remote copies, remote signals or barrier semaphores. Data moves between devices by JAX's collectives and lax.ppermute only.
A program may use at most 192 MiB of HBM per device.

```python
import math
import jax
import jax.numpy as jnp
from jax import lax

C = 32
X = 64
Y = 64
Z = 64
NT = 16
MS = 12
MT = 8
B = 2
KS = 24
KZT = 192
CC = 1024
NTC = 512


def levels(rng, dims, shards, least, high):
    loudness = 1.0
    for axis_at, parts in shards:
        draws = jax.random.uniform(jax.random.fold_in(jax.random.fold_in(rng, 6), axis_at), (parts,), jnp.float32, least / len(shards), high / len(shards))
        loudness = loudness * jnp.repeat(jnp.exp(draws), dims[axis_at] // parts).reshape((-1,) + (1,) * (len(dims) - 1 - axis_at))
    return loudness


def normal_values(key, shape, scale, most, shards=(), held_as=jnp.bfloat16):
    array = jax.random.normal(key, shape, jnp.float32) * scale
    if len(shards) > 0:
        array = levels(key, shape, shards, -0.22, 0.18) * array
    return jnp.clip(array, min=-most, max=most).astype(held_as)


def setup_inputs(seed: int = 0) -> dict:
    keys = jax.random.split(jax.random.key(seed), 6)
    inputs = normal_values(keys[0], (B, X, Y, Z, NTC), 1.0, 6.0, ((1, 16), (2, 8)))
    cotangent = normal_values(keys[1], (B, X, Y, Z, NTC), 1.0, 6.0, ((1, 16), (2, 8)))
    pre_activation = normal_values(keys[2], (B, X, Y, Z, NTC), 1.0, 6.0, ((1, 16), (2, 8)))
    pointwise = normal_values(keys[3], (C, C), C ** -0.5, 1.0)
    spectral = normal_values(keys[4], (KS, KS, KZT, CC), 0.5, 4.0, ((1, 8), (2, 16)))
    return dict(inputs=inputs, cotangent=cotangent, pre_activation=pre_activation, pointwise=pointwise, spectral=spectral)


def fourier(length, frequencies):
    points = jnp.arange(length, dtype=jnp.float32)[:, None]
    orders = jnp.arange(frequencies, dtype=jnp.float32)[None, :]
    scales = jnp.where(orders == 0.0, math.sqrt(1.0 / length), math.sqrt(2.0 / length))
    cosines = scales * jnp.cos(2.0 * math.pi * points * orders / length)
    sines = math.sqrt(2.0 / length) * jnp.sin(2.0 * math.pi * points * (orders + 1.0) / length)
    return jnp.concatenate([cosines, sines], axis=1)

def cosine(length, modes):
    points = jnp.arange(length, dtype=jnp.float32)[:, None]
    orders = jnp.arange(modes, dtype=jnp.float32)[None, :]
    scales = jnp.where(orders == 0.0, math.sqrt(1.0 / length), math.sqrt(2.0 / length))
    return scales * jnp.cos(math.pi * orders * (points + 0.5) / length)

def gelu_slope(values):
    normal_cdf = 0.5 * (1.0 + jax.scipy.special.erf(values * 0.7071067811865476))
    density = 0.3989422804014327 * jnp.exp(-0.5 * values * values)
    return normal_cdf + values * density

def reference(inputs, cotangent, pre_activation, pointwise, spectral):
    high = lax.Precision.HIGHEST
    first_basis = fourier(X, MS)
    second_basis = fourier(Y, MS)
    third_short = fourier(Z, MS).astype(jnp.bfloat16)
    time_short = cosine(NT, MT).astype(jnp.bfloat16)
    third_basis = third_short.astype(jnp.float32)
    time_basis = time_short.astype(jnp.float32)
    weights = spectral.astype(jnp.float32).reshape(KS, KS, KS, MT, C, C)

    def analysis(field):
        sectioned = jnp.einsum('xyztc,zk->xyktc', field.astype(jnp.float32), third_basis, precision=high)
        sectioned = jnp.einsum('xyktc,tm->xykmc', sectioned, time_basis, precision=high)
        sectioned = jnp.einsum('xykmc,yj->xjkmc', sectioned, second_basis, precision=high)
        return jnp.einsum('xjkmc,xi->ijkmc', sectioned, first_basis, precision=high)

    def synthesis(modes):
        sectioned = jnp.einsum('ijkmc,xi->xjkmc', modes, first_basis, precision=high)
        sectioned = jnp.einsum('xjkmc,yj->xykmc', sectioned, second_basis, precision=high)
        sectioned = jnp.einsum('xykmc,zk->xyzmc', sectioned, third_basis, precision=high)
        return jnp.einsum('xyzmc,tm->xyztc', sectioned, time_basis, precision=high)

    def sample_step(running, sample):
        field_in, field_cot, field_pre = sample
        values = field_pre.astype(jnp.float32)
        grad_flat = (field_cot.astype(jnp.float32) * gelu_slope(values)).astype(jnp.bfloat16)
        grad_pre = grad_flat.reshape(X, Y, Z, NT, C)
        input_modes = analysis(field_in.reshape(X, Y, Z, NT, C))
        grad_modes = analysis(grad_pre)
        mode_grad = jnp.einsum('ijkmco,ijkmo->ijkmc', weights, grad_modes, precision=high)
        direct = jnp.dot(grad_flat.reshape(-1, C), pointwise.T, preferred_element_type=jnp.float32)
        direct = direct.reshape(X, Y, Z, NT, C)
        input_grad = (direct + synthesis(mode_grad)).astype(jnp.bfloat16).reshape(X, Y, Z, NTC)
        outer = jnp.einsum('ijkmc,ijkmo->ijkmco', input_modes, grad_modes, precision=high)
        return (running + outer.reshape(KS, KS, KZT, CC), input_grad)
    initial = jnp.zeros((KS, KS, KZT, CC), jnp.float32)
    running, input_grad = lax.scan(sample_step, initial, (inputs, cotangent, pre_activation))
    return (input_grad, running)
```

```python
import functools
import math

import jax
import jax.numpy as jnp
import ml_dtypes
import numpy as np
from jax import lax
from jax.experimental import pallas as pl
from jax.experimental.pallas import tpu as pltpu
from jax.sharding import PartitionSpec as P

N = 64
NT = 16
MS = 12
MT = 8
KS = 24
C = 32
BF = ml_dtypes.bfloat16
F32 = jnp.float32
BF16 = jnp.bfloat16
MIB = 1 << 20


def fourier(length, frequencies):
    points = np.arange(length, dtype=np.float64)[:, None]
    orders = np.arange(frequencies, dtype=np.float64)[None, :]
    scales = np.where(orders == 0.0, math.sqrt(1.0 / length), math.sqrt(2.0 / length))
    cosines = scales * np.cos(2.0 * math.pi * points * orders / length)
    sines = math.sqrt(2.0 / length) * np.sin(2.0 * math.pi * points * (orders + 1.0) / length)
    return np.concatenate([cosines, sines], axis=1).astype(np.float32)


def cosine(length, modes):
    points = np.arange(length, dtype=np.float64)[:, None]
    orders = np.arange(modes, dtype=np.float64)[None, :]
    scales = np.where(orders == 0.0, math.sqrt(1.0 / length), math.sqrt(2.0 / length))
    return (scales * np.cos(math.pi * orders * (points + 0.5) / length)).astype(np.float32)


def constants():
    basis = fourier(N, MS)
    third = basis.astype(BF).astype(np.float32)
    time = cosine(NT, MT).astype(BF).astype(np.float32)
    eye_c = np.eye(C, dtype=np.float32)
    eye_r = np.eye(8, dtype=np.float32)
    out = {}
    tables = np.zeros((4, NT, C, 2, 4, C), np.float32)
    for pair in range(4):
        for kt in range(MT):
            half, q = divmod(kt, 4)
            tables[pair, :, :, half, (q + pair) % 4, :] = time[:, kt][:, None, None] * eye_c[None]
    tables = tables.reshape(4, NT * C, MT * C)
    out["tables"] = tables.astype(BF)
    out["tables_t"] = np.swapaxes(tables, 1, 2).copy().astype(BF)
    zl = np.einsum("zk,rs->krsz", third, eye_r).reshape(KS * 8, 8 * N)
    out["zl"] = zl.astype(BF)
    out["zl_t"] = np.concatenate([zl.T, np.zeros((8 * N, 64), np.float32)], axis=1).astype(BF)
    high = basis.astype(BF).astype(np.float32)
    low = (basis - high).astype(BF).astype(np.float32)
    eye_h = np.eye(2, dtype=np.float32)
    forms = [np.einsum("xk,hg->hkxg", part, eye_h).reshape(2 * KS, 2 * N) for part in (high, low)]
    out["xl"] = np.concatenate(forms, axis=1).astype(BF)
    out["xl_t"] = np.concatenate([form.T for form in forms], axis=1).astype(BF)
    padded = np.zeros((N, 8, 4), np.float32)
    padded[:, :, :3] = basis.reshape(N, 8, 3)
    y = padded.reshape(8, 4, 2, 32)
    yb = np.einsum("slhk,cd->hslckd", y, eye_c).reshape(2, 8 * 4 * C, 32 * C)
    out["yb"] = yb.astype(BF)
    spread = np.zeros((3, 4, C, 4, C), np.float32)
    gather = np.zeros((3, C, C, 4, C), np.float32)
    wide = np.zeros((3, 4, C, C, C), np.float32)
    for ky in range(3):
        spread[ky, ky] = eye_c[:, None, :]
        gather[ky, :, :, ky, :] = eye_c[:, None, :]
        wide[ky, ky] = eye_c[:, :, None]
    out["spread"] = spread.reshape(3, 128, 128).astype(BF)
    out["gather"] = gather.reshape(3, C * C, 128).astype(BF)
    out["wide"] = wide.reshape(3, 128, C * C).astype(BF)
    return out


def dot(a, b):
    return jnp.dot(a, b, preferred_element_type=F32)


def dot_t(a, b):
    return lax.dot_general(a, b, (((1,), (1,)), ((), ())), preferred_element_type=F32)


def gelu_slope(v):
    cdf = 0.5 * (1.0 + lax.erf(v * 0.7071067811865476))
    return cdf + v * (0.3989422804014327 * jnp.exp(-0.5 * v * v))


def lane_group(rows):
    return lax.broadcasted_iota(jnp.int32, (rows, 128), 1) // C


def analyse_field(field, table_ref, zl_ref, parts, sent_ref):
    pair = pl.program_id(1)
    timed = dot(field, table_ref[0]).astype(BF16)
    parts[pair] = dot(zl_ref[...], timed)

    @pl.when(pair == 3)
    def _():
        group = lane_group(8 * KS)
        for half in range(2):
            lanes = slice(half * 128, half * 128 + 128)
            for q in range(4):
                value = parts[(-q) % 4, :, lanes]
                for p in range(1, 4):
                    value = jnp.where(group == p, parts[(p - q) % 4, :, lanes], value)
                if q:
                    value = pltpu.roll(value, 128 - q * C, 1)
                for kz in range(KS):
                    block, slot = divmod(2 * kz + half, 3)
                    sent_ref[block, q, slot] = value[kz * 8 : kz * 8 + 8]


def analyse_grad_kernel(cot_ref, pre_ref, table_ref, zl_ref, sent_ref, grad_ref, flat, parts):
    cot = cot_ref.at[0]
    pre = pre_ref.at[0]

    def slope(i, carry):
        x, y = i // 2, i % 2
        for j in range(4):
            rows = pl.ds(j * 16, 16)
            v = pre[x, y, rows, :].astype(F32)
            g = cot[x, y, rows, :].astype(F32)
            grad = (g * gelu_slope(v)).astype(BF16)
            grad_ref[0, x, y, rows, :] = grad
            flat[pl.ds(pl.multiple_of(i * N + j * 16, 16), 16), :] = grad
        return carry

    lax.fori_loop(0, 8, slope, 0)
    analyse_field(flat[...], table_ref, zl_ref, parts, sent_ref)


def analyse_input_kernel(field_ref, table_ref, zl_ref, sent_ref, parts):
    analyse_field(field_ref[0].reshape(8 * N, NT * C), table_ref, zl_ref, parts, sent_ref)


FIELD = pl.BlockSpec((1, 4, 2, N, NT * C), lambda b, p: (b, 0, p, 0, 0))
TABLE = pl.BlockSpec((1, NT * C, MT * C), lambda b, p: (p, 0, 0))
TABLE_T = pl.BlockSpec((1, MT * C, NT * C), lambda b, p: (p, 0, 0))
SENT = pl.BlockSpec((16, 4, 3, 8, 128), lambda b, p: (0, b, 0, 0, 0))
SENT_SHAPE = jax.ShapeDtypeStruct((16, 8, 3, 8, 128), F32)
PART_SHAPE = jax.ShapeDtypeStruct((72, 128), F32)


def whole(shape):
    return pl.BlockSpec(shape, lambda *ids: (0,) * len(shape))


def params(limit):
    return pltpu.CompilerParams(vmem_limit_bytes=limit * MIB)


def analyse_grad(cotangent, pre_activation, k):
    return pl.pallas_call(
        analyse_grad_kernel,
        grid=(2, 4),
        in_specs=[FIELD, FIELD, TABLE, whole((8 * KS, 8 * N))],
        out_specs=[SENT, FIELD],
        out_shape=[SENT_SHAPE, jax.ShapeDtypeStruct(cotangent.shape, BF16)],
        scratch_shapes=[pltpu.VMEM((8 * N, NT * C), BF16), pltpu.VMEM((4, 8 * KS, MT * C), F32)],
        compiler_params=params(24),
        cost_estimate=pl.CostEstimate(flops=4 * 10**9, bytes_accessed=14 * 10**6, transcendentals=4 * 10**6),
        name="analyse_grad",
    )(cotangent, pre_activation, k["tables"], k["zl"])


def analyse_input(inputs, k):
    return pl.pallas_call(
        analyse_input_kernel,
        grid=(2, 4),
        in_specs=[FIELD, TABLE, whole((8 * KS, 8 * N))],
        out_specs=SENT,
        out_shape=SENT_SHAPE,
        scratch_shapes=[pltpu.VMEM((4, 8 * KS, MT * C), F32)],
        compiler_params=params(24),
        cost_estimate=pl.CostEstimate(flops=4 * 10**9, bytes_accessed=6 * 10**6, transcendentals=0),
        name="analyse_input",
    )(inputs, k["tables"], k["zl"])


def planes_forward_kernel(got_ref, xl_ref, yb_ref, *rest):
    outs, blocks = rest[:8], rest[8]
    me = lax.axis_index("gy")
    firsts = []
    for slot in range(3):
        field = jnp.concatenate(
            [got_ref[:, s, slot].reshape(128, 128).astype(BF16) for s in range(8)], axis=1
        )
        firsts.append(dot(xl_ref[...], jnp.concatenate([field, field], axis=0)))
    total = None
    for half in range(2):
        rows = jnp.concatenate([f[half * KS : half * KS + KS] for f in firsts], axis=0)
        term = dot(rows.astype(BF16), yb_ref[half])
        total = term if total is None else total + term
    for s in range(8):
        blocks[s] = total[:, s * 128 : s * 128 + 128]
    for s in range(8):
        outs[s][...] = blocks[me ^ s]


def planes_forward(got, k):
    return pl.pallas_call(
        planes_forward_kernel,
        out_shape=[PART_SHAPE] * 8,
        scratch_shapes=[pltpu.VMEM((8, 72, 128), F32)],
        compiler_params=params(32),
        cost_estimate=pl.CostEstimate(flops=10**9, bytes_accessed=6 * 10**6, transcendentals=0),
        name="planes_forward",
    )(got, k["xl"], k["yb"])


def planes_back_kernel(*refs):
    parts, (xl_ref, yb_ref, sent_ref, blocks) = refs[:8], refs[8:]
    me = lax.axis_index("gy")
    for s in range(8):
        blocks[me ^ s] = parts[s][...]
    field = jnp.concatenate([blocks[s] for s in range(8)], axis=1).astype(BF16)
    halves = [dot_t(field, yb_ref[half]) for half in range(2)]
    for slot in range(3):
        rows = slice(slot * KS, slot * KS + KS)
        both = jnp.concatenate([half[rows] for half in halves], axis=0).astype(BF16)
        wide = dot(xl_ref[...], jnp.concatenate([both, both], axis=0))
        for s in range(8):
            sent_ref[:, s, slot] = wide[:, s * 128 : s * 128 + 128].reshape(16, 8, 128)


def planes_back(parts, k):
    return pl.pallas_call(
        planes_back_kernel,
        out_shape=SENT_SHAPE,
        scratch_shapes=[pltpu.VMEM((8, 72, 128), F32)],
        compiler_params=params(32),
        cost_estimate=pl.CostEstimate(flops=10**9, bytes_accessed=6 * 10**6, transcendentals=0),
        name="planes_back",
    )(*parts, k["xl_t"], k["yb"])


def mode_grad_kernel(*refs):
    parts, (weight_ref, spread_ref, gather_ref), outs, products = refs[:8], refs[8:11], refs[11:19], refs[19]
    me = lax.axis_index("gy")
    field = jnp.concatenate([part[...] for part in parts], axis=0).astype(BF16)
    total = None
    for ky in range(3):
        copies = dot(field, spread_ref[ky])
        for s in range(8):
            q = (me ^ s) & 3
            for slot in range(3):
                at = s * 72 + slot * KS
                weight = weight_ref[ky, slot * 4 + q].astype(F32)
                copy = copies[at : at + KS]
                products[at : at + KS, :] = weight * jnp.concatenate([copy] * 8, axis=1)
        term = dot(products[...].astype(BF16), gather_ref[ky])
        total = term if total is None else total + term
    for s in range(8):
        outs[s][...] = total[s * 72 : s * 72 + 72]


def mode_grad(parts, weights, k):
    return pl.pallas_call(
        mode_grad_kernel,
        out_shape=[PART_SHAPE] * 8,
        scratch_shapes=[pltpu.VMEM((576, C * C), F32)],
        compiler_params=params(32),
        cost_estimate=pl.CostEstimate(flops=10**9, bytes_accessed=4 * 10**6, transcendentals=0),
        name="mode_grad",
    )(*parts, weights, k["spread"], k["gather"])


def spectral_grad_kernel(*refs):
    grads, fields, (spread_ref, wide_ref, out_ref) = refs[:8], refs[8:16], refs[16:]
    me = lax.axis_index("gy")
    grad = jnp.concatenate([part[...] for part in grads], axis=0).astype(BF16)
    field = jnp.concatenate([part[...] for part in fields], axis=0).astype(BF16)
    copies = dot(grad, spread_ref[0])
    wide = dot(field, wide_ref[0])
    for s in range(4):
        q = (me ^ s) & 3
        for slot in range(3):
            total = None
            for at in (s * 72 + slot * KS, (s + 4) * 72 + slot * KS):
                term = wide[at : at + KS] * jnp.concatenate([copies[at : at + KS]] * 8, axis=1)
                total = term if total is None else total + term
            out_ref[0, slot * 4 + q] = total


def spectral_grad(grads, fields, k):
    return pl.pallas_call(
        spectral_grad_kernel,
        grid=(3,),
        in_specs=[whole((72, 128))] * 16
        + [
            pl.BlockSpec((1, 128, 128), lambda i: (i, 0, 0)),
            pl.BlockSpec((1, 128, C * C), lambda i: (i, 0, 0)),
        ],
        out_specs=pl.BlockSpec((1, 12, KS, C * C), lambda i: (i, 0, 0, 0)),
        out_shape=jax.ShapeDtypeStruct((3, 12, KS, C * C), F32),
        compiler_params=params(32),
        cost_estimate=pl.CostEstimate(flops=10**9, bytes_accessed=4 * 10**6, transcendentals=0),
        name="spectral_grad",
    )(*grads, *fields, k["spread"], k["wide"])


def synthesise_kernel(got_ref, grad_ref, table_ref, zl_ref, mix_ref, out_ref, parts):
    pair = pl.program_id(1)

    @pl.when(pair == 0)
    def _():
        group = lane_group(8 * KS)
        for half in range(2):
            turned = []
            for q in range(4):
                tiles = []
                for kz in range(KS):
                    block, slot = divmod(2 * kz + half, 3)
                    tiles.append(got_ref[block, q, slot])
                value = jnp.concatenate(tiles, axis=0)
                turned.append(pltpu.roll(value, q * C, 1) if q else value)
            for p in range(4):
                value = turned[(-p) % 4]
                for g in range(1, 4):
                    value = jnp.where(group == g, turned[(g - p) % 4], value)
                parts[p, :, half * 128 : half * 128 + 128] = value

    timed = dot(parts[pair].astype(BF16), table_ref[0]).astype(BF16)
    timed = jnp.concatenate([timed, jnp.zeros((64, NT * C), BF16)], axis=0)
    grad = grad_ref[0].reshape(8 * N, NT * C)
    for side in range(2):
        lanes = slice(side * 256, side * 256 + 256)
        left = jnp.concatenate([zl_ref[...], grad[:, lanes]], axis=1)
        right = jnp.concatenate([timed[:, lanes], mix_ref[...]], axis=0)
        out_ref[0, :, :, :, lanes] = dot(left, right).astype(BF16).reshape(4, 2, N, 256)


def synthesise(got, grad, mix, k):
    return pl.pallas_call(
        synthesise_kernel,
        grid=(2, 4),
        in_specs=[SENT, FIELD, TABLE_T, whole((8 * N, 256)), whole((256, 256))],
        out_specs=FIELD,
        out_shape=jax.ShapeDtypeStruct(grad.shape, BF16),
        scratch_shapes=[pltpu.VMEM((4, 8 * KS, MT * C), F32)],
        compiler_params=params(24),
        cost_estimate=pl.CostEstimate(flops=4 * 10**9, bytes_accessed=10 * 10**6, transcendentals=0),
        name="synthesise",
    )(got, grad, k["tables_t"], k["zl_t"], mix)


def exchange_all(block):
    flat = block.reshape(128, 24, 128)
    return lax.all_to_all(flat, ("gx", "gy"), 0, 0, tiled=True).reshape(block.shape)


def exchange_second(parts):
    out = [parts[0]]
    for s in range(1, 8):
        out.append(lax.ppermute(parts[s], "gy", [(i, i ^ s) for i in range(8)]))
    return out


def body(inputs, cotangent, pre_activation, pointwise, spectral):
    k = constants()
    weights = jnp.transpose(spectral, (1, 2, 0, 3))
    mix = jnp.kron(jnp.eye(8, dtype=BF16), pointwise.T)
    sent, grad_pre = analyse_grad(cotangent, pre_activation, k)
    got = exchange_all(sent)
    sent_input = analyse_input(inputs, k)
    got_input = exchange_all(sent_input)
    grads = exchange_second(planes_forward(got, k))
    modes = exchange_second(mode_grad(grads, weights, k))
    back = exchange_all(planes_back(modes, k))
    fields = exchange_second(planes_forward(got_input, k))
    weight_grad = jnp.transpose(spectral_grad(grads, fields, k), (2, 0, 1, 3))
    return synthesise(back, grad_pre, mix, k), weight_grad


def solution(mesh):
    in_specs = (
        P(None, "gx", "gy", None, None),
        P(None, "gx", "gy", None, None),
        P(None, "gx", "gy", None, None),
        P(),
        P(None, "gy", "gx", None),
    )
    out_specs = (P(None, "gx", "gy", None, None), P(None, "gy", "gx", None))
    return jax.shard_map(body, mesh=mesh, in_specs=in_specs, out_specs=out_specs, check_vma=False)
```

```python
import functools
import math

import jax
import jax.numpy as jnp
import ml_dtypes
import numpy as np
from jax import lax
from jax.experimental import pallas as pl
from jax.experimental.pallas import tpu as pltpu
from jax.sharding import PartitionSpec as P

N = 64
NT = 16
MS = 12
MT = 8
KS = 24
C = 32
BF = ml_dtypes.bfloat16
F32 = jnp.float32
BF16 = jnp.bfloat16
MIB = 1 << 20


def fourier(length, frequencies):
    points = np.arange(length, dtype=np.float64)[:, None]
    orders = np.arange(frequencies, dtype=np.float64)[None, :]
    scales = np.where(orders == 0.0, math.sqrt(1.0 / length), math.sqrt(2.0 / length))
    cosines = scales * np.cos(2.0 * math.pi * points * orders / length)
    sines = math.sqrt(2.0 / length) * np.sin(2.0 * math.pi * points * (orders + 1.0) / length)
    return np.concatenate([cosines, sines], axis=1).astype(np.float32)


def cosine(length, modes):
    points = np.arange(length, dtype=np.float64)[:, None]
    orders = np.arange(modes, dtype=np.float64)[None, :]
    scales = np.where(orders == 0.0, math.sqrt(1.0 / length), math.sqrt(2.0 / length))
    return (scales * np.cos(math.pi * orders * (points + 0.5) / length)).astype(np.float32)


def constants():
    basis = fourier(N, MS)
    third = basis.astype(BF).astype(np.float32)
    time = cosine(NT, MT).astype(BF).astype(np.float32)
    eye_c = np.eye(C, dtype=np.float32)
    eye_r = np.eye(8, dtype=np.float32)
    out = {}
    tables = np.zeros((4, NT, C, 2, 4, C), np.float32)
    for pair in range(4):
        for kt in range(MT):
            half, q = divmod(kt, 4)
            tables[pair, :, :, half, (q + pair) % 4, :] = time[:, kt][:, None, None] * eye_c[None]
    tables = tables.reshape(4, NT * C, MT * C)
    out["tables"] = tables.astype(BF)
    out["tables_t"] = np.swapaxes(tables, 1, 2).copy().astype(BF)
    zl = np.einsum("zk,rs->krsz", third, eye_r).reshape(KS * 8, 8 * N)
    out["zl"] = zl.astype(BF)
    out["zl_t"] = np.concatenate([zl.T, np.zeros((8 * N, 64), np.float32)], axis=1).astype(BF)
    high = basis.astype(BF).astype(np.float32)
    low = (basis - high).astype(BF).astype(np.float32)
    eye_h = np.eye(2, dtype=np.float32)
    forms = [np.einsum("xk,hg->hkxg", part, eye_h).reshape(2 * KS, 2 * N) for part in (high, low)]
    out["xl"] = np.concatenate(forms, axis=1).astype(BF)
    out["xl_t"] = np.concatenate([form.T for form in forms], axis=1).astype(BF)
    second = basis.reshape(8, 4, 2, 8, 3)
    out["cy"] = np.repeat(np.einsum("slhdj->djhsl", second).reshape(8, 3, 16, 4), C, axis=3)
    spread = np.zeros((3, 4, C, 4, C), np.float32)
    gather = np.zeros((3, C, C, 4, C), np.float32)
    wide = np.zeros((3, 4, C, C, C), np.float32)
    for ky in range(3):
        spread[ky, ky] = eye_c[:, None, :]
        gather[ky, :, :, ky, :] = eye_c[:, None, :]
        wide[ky, ky] = eye_c[:, :, None]
    out["spread"] = spread.reshape(3, 128, 128).astype(BF)
    out["gather"] = gather.reshape(3, C * C, 128).astype(BF)
    out["wide"] = wide.reshape(3, 128, C * C).astype(BF)
    return out


def dot(a, b):
    return jnp.dot(a, b, preferred_element_type=F32)


def gelu_slope(v):
    cdf = 0.5 * (1.0 + lax.erf(v * 0.7071067811865476))
    return cdf + v * (0.3989422804014327 * jnp.exp(-0.5 * v * v))


def lane_group(rows):
    return lax.broadcasted_iota(jnp.int32, (rows, 128), 1) // C


def send_parts(parts, sent_ref):
    group = lane_group(8 * KS)
    for half in range(2):
        lanes = slice(half * 128, half * 128 + 128)
        for q in range(4):
            value = parts[(-q) % 4, :, lanes]
            for p in range(1, 4):
                value = jnp.where(group == p, parts[(p - q) % 4, :, lanes], value)
            if q:
                value = pltpu.roll(value, 128 - q * C, 1)
            for kz in range(KS):
                block, slot = divmod(2 * kz + half, 3)
                sent_ref[block, q, slot] = value[kz * 8 : kz * 8 + 8]


def analyse_grad_kernel(cot_ref, pre_ref, table_ref, zl_ref, sent_ref, grad_ref, flat, timed, parts):
    step = pl.program_id(1)

    def time(n, carry):
        timed[n] = dot(flat[n & 1], table_ref[n // 4]).astype(BF16)
        return carry

    def slope(n, carry):
        pair, x = n // 4, n % 4
        before = jnp.maximum(n - 1, 0)
        earlier = dot(flat[(n + 1) & 1], table_ref[before // 4])
        for y in range(2):
            for j in range(4):
                rows = pl.ds(j * 16, 16)
                v = pre_ref[0, x, 2 * pair + y, rows, :].astype(F32)
                g = cot_ref[0, x, 2 * pair + y, rows, :].astype(F32)
                grad = (g * gelu_slope(v)).astype(BF16)
                grad_ref[0, x, 2 * pair + y, rows, :] = grad
                flat[n & 1, y * N + j * 16 : y * N + j * 16 + 16, :] = grad
        timed[before] = earlier.astype(BF16)
        return carry

    lax.fori_loop(0, 8, slope, 0)
    time(7, 0)
    for pair in range(2):
        parts[2 * step + pair] = dot(zl_ref[...], timed[4 * pair : 4 * pair + 4].reshape(8 * N, MT * C))

    @pl.when(step == 1)
    def _():
        send_parts(parts, sent_ref)


def analyse_input_kernel(field_ref, table_ref, zl_ref, sent_ref, parts):
    step = pl.program_id(1)
    for pair in range(2):
        field = field_ref[0, :, 2 * pair : 2 * pair + 2].reshape(8 * N, NT * C)
        timed = dot(field, table_ref[pair]).astype(BF16)
        parts[2 * step + pair] = dot(zl_ref[...], timed)

    @pl.when(step == 1)
    def _():
        send_parts(parts, sent_ref)


FIELD = pl.BlockSpec((1, 4, 4, N, NT * C), lambda b, p: (b, 0, p, 0, 0))
TABLE = pl.BlockSpec((2, NT * C, MT * C), lambda b, p: (p, 0, 0))
TABLE_T = pl.BlockSpec((2, MT * C, NT * C), lambda b, p: (p, 0, 0))
SENT = pl.BlockSpec((16, 4, 3, 8, 128), lambda b, p: (0, b, 0, 0, 0))
SENT_SHAPE = (16, 8, 3, 8, 128)
PART, PLANE = 72, 144
ANY = pl.BlockSpec(memory_space=pl.ANY)


def whole(shape):
    return pl.BlockSpec(shape, lambda *ids: (0,) * len(shape))


def params(limit):
    return pltpu.CompilerParams(vmem_limit_bytes=limit * MIB)


def cost(flops, nbytes):
    return pl.CostEstimate(flops=flops, bytes_accessed=nbytes, transcendentals=0)


def in_hbm(*arrays):
    return [pltpu.with_memory_space_constraint(a, pltpu.HBM) for a in arrays]


def analyse_grad(cotangent, pre_activation, k):
    return pl.pallas_call(
        analyse_grad_kernel,
        grid=(2, 2),
        in_specs=[FIELD, FIELD, TABLE, whole((8 * KS, 8 * N))],
        out_specs=[SENT, FIELD],
        out_shape=[pltpu.HBM(SENT_SHAPE, F32), pltpu.HBM(cotangent.shape, BF16)],
        scratch_shapes=[
            pltpu.VMEM((2, 2 * N, NT * C), BF16),
            pltpu.VMEM((8, 2 * N, MT * C), BF16),
            pltpu.VMEM((4, 8 * KS, MT * C), F32),
        ],
        compiler_params=params(24),
        cost_estimate=cost(4 * 10**9, 14 * 10**6),
        name="analyse_grad",
    )(*in_hbm(cotangent, pre_activation, k["tables"], k["zl"]))


def analyse_input(inputs, k):
    return pl.pallas_call(
        analyse_input_kernel,
        grid=(2, 2),
        in_specs=[FIELD, TABLE, whole((8 * KS, 8 * N))],
        out_specs=SENT,
        out_shape=pltpu.HBM(SENT_SHAPE, F32),
        scratch_shapes=[pltpu.VMEM((4, 8 * KS, MT * C), F32)],
        compiler_params=params(24),
        cost_estimate=cost(4 * 10**9, 6 * 10**6),
        name="analyse_input",
    )(*in_hbm(inputs, k["tables"], k["zl"]))


def transform_x(got_ref, xl_ref, planes):
    for slot in range(3):
        field = jnp.concatenate(
            [got_ref[:, s, slot].reshape(128, 128).astype(BF16) for s in range(8)], axis=1
        )
        wide = dot(xl_ref[...], jnp.concatenate([field, field], axis=0))
        for s in range(8):
            planes[s, slot * 48 : slot * 48 + 48, :] = wide[:, s * 128 : s * 128 + 128]


def transform_y(planes, cy_ref, blocks):
    group = lane_group(72)

    def block(d, carry):
        totals = [jnp.zeros((72, 128), F32)] * 3
        for s in range(8):
            for half in range(2):
                starts = [slot * 48 + half * KS for slot in range(3)]
                rows = jnp.concatenate([planes[s, at : at + KS, :] for at in starts], axis=0)
                for j in range(3):
                    totals[j] = totals[j] + rows * cy_ref[d, j, half * 8 + s : half * 8 + s + 1, :]
        value = jnp.zeros((72, 128), F32)
        for j in range(3):
            total = totals[j] + pltpu.roll(totals[j], 64, 1)
            total = total + pltpu.roll(total, 32, 1)
            value = jnp.where(group == j, total, value)
        blocks[d] = value
        return carry

    lax.fori_loop(0, 8, block, 0)


def group_shape(rows):
    return jax.ShapeDtypeStruct((4, rows, 128), F32)


def deal(blocks, keep_ref, cross_ref):
    me = lax.axis_index("gy")
    for sx in range(4):
        keep_ref[sx] = blocks[me ^ (2 * sx)]
        cross_ref[sx] = blocks[me ^ (2 * sx + 1)]


def arrived(refs):
    keep, cross, *far = refs
    return [keep.at[0], cross.at[0]] + [ref.at[i] for ref in far for i in range(2)]


def collect(parts, blocks):
    me = lax.axis_index("gy")
    for s in range(8):
        blocks[me ^ s] = parts[s][...]


def planes_forward_kernel(got_ref, xl_ref, cy_ref, *rest):
    keep_ref, cross_ref, planes, blocks = rest
    transform_x(got_ref, xl_ref, planes)
    transform_y(planes, cy_ref, blocks)
    deal(blocks, keep_ref, cross_ref)


def planes_forward(got, xl, cy):
    return pl.pallas_call(
        planes_forward_kernel,
        out_shape=[group_shape(PART)] * 2,
        scratch_shapes=[pltpu.VMEM((8, PLANE, 128), F32), pltpu.VMEM((8, PART, 128), F32)],
        compiler_params=params(16),
        cost_estimate=cost(10**9, 3 * 10**6),
        name="planes_forward",
    )(got, xl, cy)


def planes_x_kernel(got_ref, xl_ref, keep_ref, cross_ref, planes):
    transform_x(got_ref, xl_ref, planes)
    deal(planes, keep_ref, cross_ref)


def planes_x(got, xl):
    return pl.pallas_call(
        planes_x_kernel,
        out_shape=[group_shape(PLANE)] * 2,
        scratch_shapes=[pltpu.VMEM((8, PLANE, 128), F32)],
        compiler_params=params(16),
        cost_estimate=cost(10**9, 2 * 10**6),
        name="planes_x",
    )(got, xl)


def planes_y_kernel(*refs):
    parts, (cy_ref, keep_ref, cross_ref, planes, blocks) = arrived(refs[:5]), refs[5:]
    collect(parts, planes)
    transform_y(planes, cy_ref, blocks)
    deal(blocks, keep_ref, cross_ref)


def planes_y(parts, cy):
    return pl.pallas_call(
        planes_y_kernel,
        out_shape=[group_shape(PART)] * 2,
        scratch_shapes=[pltpu.VMEM((8, PLANE, 128), F32), pltpu.VMEM((8, PART, 128), F32)],
        compiler_params=params(16),
        cost_estimate=cost(10**9, 2 * 10**6),
        name="planes_y",
    )(*parts, cy)


def back_y_kernel(*refs):
    parts, (cy_ref, spread_ref, keep_ref, cross_ref, blocks, copies, planes) = arrived(refs[:5]), refs[5:]
    collect(parts, blocks)
    field = blocks[...].reshape(576, 128).astype(BF16)
    for j in range(3):
        copies[j] = dot(field, spread_ref[j])

    def plane(s, carry):
        totals = [jnp.zeros((72, 128), F32)] * 2
        for d in range(8):
            for j in range(3):
                rows = copies[j, d * 72 : d * 72 + 72, :]
                for half in range(2):
                    totals[half] = totals[half] + rows * cy_ref[d, j, pl.ds(half * 8 + s, 1), :]
        for half in range(2):
            for slot in range(3):
                at = slot * 48 + half * KS
                planes[s, at : at + KS, :] = totals[half][slot * KS : slot * KS + KS]
        return carry

    lax.fori_loop(0, 8, plane, 0)
    deal(planes, keep_ref, cross_ref)


def back_y(parts, cy, spread):
    return pl.pallas_call(
        back_y_kernel,
        out_shape=[group_shape(PLANE)] * 2,
        scratch_shapes=[
            pltpu.VMEM((8, PART, 128), F32),
            pltpu.VMEM((3, 8 * PART, 128), F32),
            pltpu.VMEM((8, PLANE, 128), F32),
        ],
        compiler_params=params(16),
        cost_estimate=cost(10**9, 2 * 10**6),
        name="back_y",
    )(*parts, cy, spread)


def back_x_kernel(*refs):
    parts, (xl_ref, sent_ref, planes) = arrived(refs[:5]), refs[5:]
    collect(parts, planes)
    for slot in range(3):
        rows = slice(slot * 48, slot * 48 + 48)
        both = jnp.concatenate([planes[s, rows, :] for s in range(8)], axis=1).astype(BF16)
        wide = dot(xl_ref[...], jnp.concatenate([both, both], axis=0))
        for s in range(8):
            sent_ref[:, s, slot] = wide[:, s * 128 : s * 128 + 128].reshape(16, 8, 128)


def back_x(parts, xl_t):
    return pl.pallas_call(
        back_x_kernel,
        out_shape=pltpu.HBM(SENT_SHAPE, F32),
        out_specs=pl.BlockSpec(SENT_SHAPE, lambda: (0,) * 5),
        scratch_shapes=[pltpu.VMEM((8, PLANE, 128), F32)],
        compiler_params=params(16),
        cost_estimate=cost(10**9, 2 * 10**6),
        name="back_x",
    )(*parts, xl_t)


def pair_up_kernel(keep_ref, cross_ref, *outs):
    for sx in range(1, 4):
        outs[sx - 1][0] = keep_ref[sx]
        outs[sx - 1][1] = cross_ref[sx]


def pair_up(keep, cross):
    shape = jax.ShapeDtypeStruct((2, *keep.shape[1:]), F32)
    return pl.pallas_call(
        pair_up_kernel,
        out_shape=[shape] * 3,
        compiler_params=params(16),
        cost_estimate=cost(10**6, 10**6),
        name="pair_up",
    )(keep, cross)


def exchange_second(blocks):
    keep, cross = blocks
    cross = lax.ppermute(cross, "gy", [(i, i ^ 1) for i in range(8)])
    pairs = pair_up(keep, cross)
    far = [lax.ppermute(pairs[sx - 1], "gy", [(i, i ^ (2 * sx)) for i in range(8)]) for sx in range(1, 4)]
    return [keep, cross] + far


def mode_grad_kernel(*refs):
    parts, (spread_ref, weight_hbm, gather_hbm, keep_ref, cross_ref) = arrived(refs[:5]), refs[5:10]
    products, weight_ref, gather_ref, sems = refs[10:]
    copies = []
    for ky in range(3):
        copies.append(
            (
                pltpu.make_async_copy(weight_hbm.at[ky], weight_ref.at[ky], sems.at[0, ky]),
                pltpu.make_async_copy(gather_hbm.at[ky], gather_ref.at[ky], sems.at[1, ky]),
            )
        )
    for weight, gather in copies:
        weight.start()
        gather.start()
    me = lax.axis_index("gy")
    field = jnp.concatenate([part[...] for part in parts], axis=0).astype(BF16)
    total = None
    for ky in range(3):
        lanes = dot(field, spread_ref[ky])
        copies[ky][0].wait()
        for s in range(8):
            q = (me ^ s) & 3
            for slot in range(3):
                at = s * 72 + slot * KS
                weight = weight_ref[ky, slot * 4 + q].astype(F32)
                products[at : at + KS, :] = weight * jnp.concatenate([lanes[at : at + KS]] * 8, axis=1)
        copies[ky][1].wait()
        term = dot(products[...].astype(BF16), gather_ref[ky])
        total = term if total is None else total + term
    for sx in range(4):
        keep_ref[sx] = total[2 * sx * 72 : 2 * sx * 72 + 72]
        cross_ref[sx] = total[(2 * sx + 1) * 72 : (2 * sx + 1) * 72 + 72]


def mode_grad(parts, weights, k):
    vmem = pl.BlockSpec(memory_space=pltpu.VMEM)
    return pl.pallas_call(
        mode_grad_kernel,
        in_specs=[vmem] * 6 + [ANY] * 2,
        out_shape=[group_shape(PART)] * 2,
        scratch_shapes=[
            pltpu.VMEM((576, C * C), F32),
            pltpu.VMEM(weights.shape, BF16),
            pltpu.VMEM((3, C * C, 128), BF16),
            pltpu.SemaphoreType.DMA((2, 3)),
        ],
        compiler_params=params(16),
        cost_estimate=cost(10**9, 4 * 10**6),
        name="mode_grad",
    )(*parts, k["spread"], *in_hbm(weights, k["gather"]))


def spectral_grad_kernel(*refs):
    grads, fields, (spread_ref, wide_ref, out_ref) = arrived(refs[:5]), arrived(refs[5:10]), refs[10:]
    me = lax.axis_index("gy")
    grad = jnp.concatenate([part[...] for part in grads], axis=0).astype(BF16)
    field = jnp.concatenate([part[...] for part in fields], axis=0).astype(BF16)
    copies = dot(grad, spread_ref[0])
    wide = dot(field, wide_ref[0])
    for s in range(4):
        q = (me ^ s) & 3
        for slot in range(3):
            total = None
            for at in (s * 72 + slot * KS, (s + 4) * 72 + slot * KS):
                term = wide[at : at + KS] * jnp.concatenate([copies[at : at + KS]] * 8, axis=1)
                total = term if total is None else total + term
            out_ref[0, slot * 4 + q] = total


def spectral_grad(grads, fields, spread, wide):
    return pl.pallas_call(
        spectral_grad_kernel,
        grid=(3,),
        in_specs=[whole((4, PART, 128))] * 2
        + [whole((2, PART, 128))] * 3
        + [whole((4, PART, 128))] * 2
        + [whole((2, PART, 128))] * 3
        + [
            pl.BlockSpec((1, 128, 128), lambda i: (i, 0, 0)),
            pl.BlockSpec((1, 128, C * C), lambda i: (i, 0, 0)),
        ],
        out_specs=pl.BlockSpec((1, 12, KS, C * C), lambda i: (i, 0, 0, 0)),
        out_shape=pltpu.HBM((3, 12, KS, C * C), F32),
        compiler_params=params(24),
        cost_estimate=cost(10**9, 4 * 10**6),
        name="spectral_grad",
    )(*grads, *fields, *in_hbm(spread, wide))


def synthesise_kernel(got_ref, grad_ref, table_ref, zl_ref, mix_ref, out_ref, parts):
    step = pl.program_id(1)

    @pl.when(step == 0)
    def _():
        group = lane_group(8 * KS)
        for half in range(2):
            turned = []
            for q in range(4):
                tiles = []
                for kz in range(KS):
                    block, slot = divmod(2 * kz + half, 3)
                    tiles.append(got_ref[block, q, slot])
                value = jnp.concatenate(tiles, axis=0)
                turned.append(pltpu.roll(value, q * C, 1) if q else value)
            for p in range(4):
                value = turned[(-p) % 4]
                for g in range(1, 4):
                    value = jnp.where(group == g, turned[(g - p) % 4], value)
                parts[p, :, half * 128 : half * 128 + 128] = value.astype(BF16)

    for pair in range(2):
        timed = dot(parts[2 * step + pair], table_ref[pair]).astype(BF16)
        timed = jnp.concatenate([timed, jnp.zeros((64, NT * C), BF16)], axis=0)
        ys = slice(2 * pair, 2 * pair + 2)
        grad = grad_ref[0, :, ys].reshape(8 * N, NT * C)
        for side in range(2):
            lanes = slice(side * 256, side * 256 + 256)
            left = jnp.concatenate([zl_ref[...], grad[:, lanes]], axis=1)
            right = jnp.concatenate([timed[:, lanes], mix_ref[...]], axis=0)
            out_ref[0, :, ys, :, lanes] = dot(left, right).astype(BF16).reshape(4, 2, N, 256)


def synthesise(got, grad, mix, k):
    return pl.pallas_call(
        synthesise_kernel,
        grid=(2, 2),
        in_specs=[SENT, FIELD, TABLE_T, whole((8 * N, 256)), whole((256, 256))],
        out_specs=FIELD,
        out_shape=pltpu.HBM(grad.shape, BF16),
        scratch_shapes=[pltpu.VMEM((4, 8 * KS, MT * C), BF16)],
        compiler_params=params(24),
        cost_estimate=cost(4 * 10**9, 10 * 10**6),
        name="synthesise",
    )(got, *in_hbm(grad, k["tables_t"], k["zl_t"], mix))


def exchange_all(block):
    flat = block.reshape(128, 24, 128)
    return lax.all_to_all(flat, ("gx", "gy"), 0, 0, tiled=True).reshape(block.shape)


def exchange_first(block):
    flat = block.reshape(16, 192, 128)
    return lax.all_to_all(flat, "gx", 0, 0, tiled=True).reshape(block.shape)


def body(inputs, cotangent, pre_activation, pointwise, spectral):
    k = constants()
    xl, cy, spread = k["xl"], k["cy"], k["spread"]
    weights = jnp.transpose(spectral, (1, 2, 0, 3))
    mix = jnp.kron(jnp.eye(8, dtype=BF16), pointwise.T)
    sent, grad_pre = analyse_grad(cotangent, pre_activation, k)
    got = exchange_all(sent)
    got_input = exchange_first(analyse_input(inputs, k))
    grads = exchange_second(planes_forward(got, xl, cy))
    modes = exchange_second(mode_grad(grads, weights, k))
    back = exchange_first(back_x(exchange_second(back_y(modes, cy, spread)), k["xl_t"]))
    planes = exchange_second(planes_x(got_input, xl))
    fields = exchange_second(planes_y(planes, cy))
    weight_grad = spectral_grad(grads, fields, spread, k["wide"])
    return synthesise(back, grad_pre, mix, k), jnp.transpose(weight_grad, (2, 0, 1, 3))


def solution(mesh):
    in_specs = (
        P(None, "gx", "gy", None, None),
        P(None, "gx", "gy", None, None),
        P(None, "gx", "gy", None, None),
        P(),
        P(None, "gy", "gx", None),
    )
    out_specs = (P(None, "gx", "gy", None, None), P(None, "gy", "gx", None))
    return jax.shard_map(body, mesh=mesh, in_specs=in_specs, out_specs=out_specs, check_vma=False)
```

```python
import functools
import math

import jax
import jax.numpy as jnp
import ml_dtypes
import numpy as np
from jax import lax
from jax.experimental import pallas as pl
from jax.experimental.pallas import tpu as pltpu
from jax.sharding import PartitionSpec as P

N = 64
NT = 16
MS = 12
MT = 8
KS = 24
C = 32
BF = ml_dtypes.bfloat16
F32 = jnp.float32
BF16 = jnp.bfloat16
MIB = 1 << 20


def fourier(length, frequencies):
    points = np.arange(length, dtype=np.float64)[:, None]
    orders = np.arange(frequencies, dtype=np.float64)[None, :]
    scales = np.where(orders == 0.0, math.sqrt(1.0 / length), math.sqrt(2.0 / length))
    cosines = scales * np.cos(2.0 * math.pi * points * orders / length)
    sines = math.sqrt(2.0 / length) * np.sin(2.0 * math.pi * points * (orders + 1.0) / length)
    return np.concatenate([cosines, sines], axis=1).astype(np.float32)


def cosine(length, modes):
    points = np.arange(length, dtype=np.float64)[:, None]
    orders = np.arange(modes, dtype=np.float64)[None, :]
    scales = np.where(orders == 0.0, math.sqrt(1.0 / length), math.sqrt(2.0 / length))
    return (scales * np.cos(math.pi * orders * (points + 0.5) / length)).astype(np.float32)


def constants():
    basis = fourier(N, MS)
    third = basis.astype(BF).astype(np.float32)
    time = cosine(NT, MT).astype(BF).astype(np.float32)
    eye_c = np.eye(C, dtype=np.float32)
    eye_r = np.eye(8, dtype=np.float32)
    out = {}
    tables = np.zeros((4, NT, C, 2, 4, C), np.float32)
    for pair in range(4):
        for kt in range(MT):
            half, q = divmod(kt, 4)
            tables[pair, :, :, half, (q + pair) % 4, :] = time[:, kt][:, None, None] * eye_c[None]
    tables = tables.reshape(4, NT * C, MT * C)
    out["tables"] = tables.astype(BF)
    out["tables_t"] = np.swapaxes(tables, 1, 2).copy().astype(BF)
    zl = np.einsum("zk,rs->krsz", third, eye_r).reshape(KS * 8, 8 * N)
    out["zl"] = zl.astype(BF)
    out["zl_t"] = np.concatenate([zl.T, np.zeros((8 * N, 64), np.float32)], axis=1).astype(BF)
    high = basis.astype(BF).astype(np.float32)
    low = (basis - high).astype(BF).astype(np.float32)
    eye_h = np.eye(2, dtype=np.float32)
    forms = [np.einsum("xk,hg->hkxg", part, eye_h).reshape(2 * KS, 2 * N) for part in (high, low)]
    out["xl"] = np.concatenate(forms, axis=1).astype(BF)
    out["xl_t"] = np.concatenate([form.T for form in forms], axis=1).astype(BF)
    padded = np.zeros((N, 8, 4), np.float32)
    padded[:, :, :3] = basis.reshape(N, 8, 3)
    yb = np.einsum("slhdk,ce->shlcdke", padded.reshape(8, 4, 2, 8, 4), eye_c)
    out["yb"] = yb.reshape(8, 256, 1024).astype(BF)
    second = basis.reshape(8, 4, 2, 8, 3)
    out["cy"] = np.repeat(np.einsum("slhdj->djhsl", second).reshape(8, 3, 16, 4), C, axis=3)
    spread = np.zeros((4, 4, C, 4, C), np.float32)
    gather = np.zeros((4, C, C, 4, C), np.float32)
    wide = np.zeros((4, 4, C, C, C), np.float32)
    for j in range(4):
        spread[j, j] = eye_c[:, None, :]
        gather[j, :, :, j, :] = eye_c[:, None, :]
        wide[j, j] = eye_c[:, :, None]
    out["spread"] = spread.reshape(4, 128, 128).astype(BF)
    out["gather"] = gather.reshape(4, C * C, 128).astype(BF)
    out["wide"] = wide.reshape(4, 128, C * C).astype(BF)
    return out


def dot(a, b):
    return jnp.dot(a, b, preferred_element_type=F32)


def dot_t(a, b):
    return lax.dot_general(a, b, (((1,), (1,)), ((), ())), preferred_element_type=F32)


def gelu_slope(v):
    cdf = 0.5 * (1.0 + lax.erf(v * 0.7071067811865476))
    return cdf + v * (0.3989422804014327 * jnp.exp(-0.5 * v * v))


def lane_group(rows):
    return lax.broadcasted_iota(jnp.int32, (rows, 128), 1) // C


def send_parts(parts, sent_ref):
    group = lane_group(8 * KS)
    for half in range(2):
        lanes = slice(half * 128, half * 128 + 128)
        for q in range(4):
            value = parts[(-q) % 4, :, lanes]
            for p in range(1, 4):
                value = jnp.where(group == p, parts[(p - q) % 4, :, lanes], value)
            if q:
                value = pltpu.roll(value, 128 - q * C, 1)
            for kz in range(KS):
                block, slot = divmod(2 * kz + half, 3)
                sent_ref[block, q, slot] = value[kz * 8 : kz * 8 + 8]


def analyse_grad_kernel(cot_ref, pre_ref, table_ref, zl_ref, sent_ref, grad_ref, flat, timed, parts):
    step = pl.program_id(1)

    def time(n, carry):
        timed[n] = dot(flat[n & 1], table_ref[n // 4]).astype(BF16)
        return carry

    def slope(n, carry):
        pair, x = n // 4, n % 4
        before = jnp.maximum(n - 1, 0)
        earlier = dot(flat[(n + 1) & 1], table_ref[before // 4])
        for y in range(2):
            for j in range(4):
                rows = pl.ds(j * 16, 16)
                v = pre_ref[0, x, 2 * pair + y, rows, :].astype(F32)
                g = cot_ref[0, x, 2 * pair + y, rows, :].astype(F32)
                grad = (g * gelu_slope(v)).astype(BF16)
                grad_ref[0, x, 2 * pair + y, rows, :] = grad
                flat[n & 1, y * N + j * 16 : y * N + j * 16 + 16, :] = grad
        timed[before] = earlier.astype(BF16)
        return carry

    lax.fori_loop(0, 8, slope, 0)
    time(7, 0)
    for pair in range(2):
        parts[2 * step + pair] = dot(zl_ref[...], timed[4 * pair : 4 * pair + 4].reshape(8 * N, MT * C))

    @pl.when(step == 1)
    def _():
        send_parts(parts, sent_ref)


def analyse_input_kernel(field_ref, table_ref, zl_ref, sent_ref, parts):
    step = pl.program_id(1)
    for pair in range(2):
        field = field_ref[0, :, 2 * pair : 2 * pair + 2].reshape(8 * N, NT * C)
        timed = dot(field, table_ref[pair]).astype(BF16)
        parts[2 * step + pair] = dot(zl_ref[...], timed)

    @pl.when(step == 1)
    def _():
        send_parts(parts, sent_ref)


FIELD = pl.BlockSpec((1, 4, 4, N, NT * C), lambda b, p: (b, 0, p, 0, 0))
TABLE = pl.BlockSpec((2, NT * C, MT * C), lambda b, p: (p, 0, 0))
TABLE_T = pl.BlockSpec((2, MT * C, NT * C), lambda b, p: (p, 0, 0))
SENT = pl.BlockSpec((16, 4, 3, 8, 128), lambda b, p: (0, b, 0, 0, 0))
SENT_SHAPE = (16, 8, 3, 8, 128)
TILES = (6, 72, 128)
ANY = pl.BlockSpec(memory_space=pl.ANY)


def whole(shape):
    return pl.BlockSpec(shape, lambda *ids: (0,) * len(shape))


def params(limit):
    return pltpu.CompilerParams(vmem_limit_bytes=limit * MIB)


def cost(flops, nbytes):
    return pl.CostEstimate(flops=flops, bytes_accessed=nbytes, transcendentals=0)


def in_hbm(*arrays):
    return [pltpu.with_memory_space_constraint(a, pltpu.HBM) for a in arrays]


def analyse_grad(cotangent, pre_activation, k):
    return pl.pallas_call(
        analyse_grad_kernel,
        grid=(2, 2),
        in_specs=[FIELD, FIELD, TABLE, whole((8 * KS, 8 * N))],
        out_specs=[SENT, FIELD],
        out_shape=[pltpu.HBM(SENT_SHAPE, F32), pltpu.HBM(cotangent.shape, BF16)],
        scratch_shapes=[
            pltpu.VMEM((2, 2 * N, NT * C), BF16),
            pltpu.VMEM((8, 2 * N, MT * C), BF16),
            pltpu.VMEM((4, 8 * KS, MT * C), F32),
        ],
        compiler_params=params(24),
        cost_estimate=cost(4 * 10**9, 14 * 10**6),
        name="analyse_grad",
    )(*in_hbm(cotangent, pre_activation, k["tables"], k["zl"]))


def analyse_input(inputs, k):
    return pl.pallas_call(
        analyse_input_kernel,
        grid=(2, 2),
        in_specs=[FIELD, TABLE, whole((8 * KS, 8 * N))],
        out_specs=SENT,
        out_shape=pltpu.HBM(SENT_SHAPE, F32),
        scratch_shapes=[pltpu.VMEM((4, 8 * KS, MT * C), F32)],
        compiler_params=params(24),
        cost_estimate=cost(4 * 10**9, 6 * 10**6),
        name="analyse_input",
    )(*in_hbm(inputs, k["tables"], k["zl"]))


def mode_of(j, t):
    return (j, t) if j < 3 else (t, 3)


def forward_kernel(got_ref, xl_ref, yb_hbm, keep_ref, cross_ref, yb_ref, fields, blocks, sem):
    me = lax.axis_index("gy")
    copy = pltpu.make_async_copy(yb_hbm.at[me], yb_ref, sem)
    copy.start()
    for slot in range(3):
        field = jnp.concatenate(
            [got_ref[:, d, slot].reshape(128, 128).astype(BF16) for d in range(8)], axis=1
        )
        wide = dot(xl_ref[...], jnp.concatenate([field, field], axis=0))
        for d in range(8):
            for half in range(2):
                rows = slice(d * 72 + slot * KS, d * 72 + slot * KS + KS)
                fields[rows, half * 128 : half * 128 + 128] = wide[
                    half * KS : half * KS + KS, d * 128 : d * 128 + 128
                ]
    copy.wait()
    group = lane_group(72)
    field = fields[...].astype(BF16)
    for to in range(8):
        part = dot(field, yb_ref[:, to * 128 : to * 128 + 128])
        for b in range(2):
            last = part[(4 * b + 3) * 72 : (4 * b + 4) * 72]
            for t in range(3):
                value = part[(4 * b + t) * 72 : (4 * b + t + 1) * 72]
                blocks[to, 3 * b + t] = jnp.where(group == 3, pltpu.roll(last, 96 - 32 * t, 1), value)
    for sx in range(4):
        keep_ref[sx] = blocks[me ^ (2 * sx)]
        cross_ref[sx] = blocks[me ^ (2 * sx + 1)]


def forward(got, k):
    vmem = pl.BlockSpec(memory_space=pltpu.VMEM)
    return pl.pallas_call(
        forward_kernel,
        in_specs=[vmem, vmem, ANY],
        out_shape=[jax.ShapeDtypeStruct((4, *TILES), F32)] * 2,
        scratch_shapes=[
            pltpu.VMEM((256, 1024), BF16),
            pltpu.VMEM((576, 256), F32),
            pltpu.VMEM((8, *TILES), F32),
            pltpu.SemaphoreType.DMA,
        ],
        compiler_params=params(16),
        cost_estimate=cost(10**9, 4 * 10**6),
        name="forward",
    )(got, k["xl"], *in_hbm(k["yb"]))


def add_cores_kernel(keep_ref, cross_ref, *outs):
    for sx in range(4):
        outs[sx][...] = keep_ref[sx] + cross_ref[sx]


def add_cores(keep, cross):
    return pl.pallas_call(
        add_cores_kernel,
        out_shape=[jax.ShapeDtypeStruct(TILES, F32)] * 4,
        compiler_params=params(16),
        cost_estimate=cost(10**6, 10**6),
        name="add_cores",
    )(keep, cross)


def across(block, sx):
    return lax.ppermute(block, "gy", [(i, i ^ sx) for i in range(8)])


def reduce_cores(blocks):
    keep, cross = blocks
    return add_cores(keep, across(cross, 1))


def reduce_chips(sums):
    own, *others = sums
    return [own] + [across(other, 2 * sx + 2) for sx, other in enumerate(others)]


def gather_second(block):
    parts = [block, across(block, 1)]
    for sx in range(1, 4):
        far = across(block, 2 * sx)
        parts += [far, across(far, 1)]
    return parts


def transform_x(got_ref, xl_ref, planes):
    for slot in range(3):
        field = jnp.concatenate(
            [got_ref[:, s, slot].reshape(128, 128).astype(BF16) for s in range(8)], axis=1
        )
        wide = dot(xl_ref[...], jnp.concatenate([field, field], axis=0))
        for s in range(8):
            planes[s, slot * 48 : slot * 48 + 48, :] = wide[:, s * 128 : s * 128 + 128]


def transform_y(planes, cy_ref, blocks):
    group = lane_group(72)

    def block(d, carry):
        totals = [jnp.zeros((72, 128), F32)] * 3
        for s in range(8):
            for half in range(2):
                starts = [slot * 48 + half * KS for slot in range(3)]
                rows = jnp.concatenate([planes[s, at : at + KS, :] for at in starts], axis=0)
                for j in range(3):
                    totals[j] = totals[j] + rows * cy_ref[d, j, half * 8 + s : half * 8 + s + 1, :]
        value = jnp.zeros((72, 128), F32)
        for j in range(3):
            total = totals[j] + pltpu.roll(totals[j], 64, 1)
            total = total + pltpu.roll(total, 32, 1)
            value = jnp.where(group == j, total, value)
        blocks[d] = value
        return carry

    lax.fori_loop(0, 8, block, 0)


def group_shape(rows):
    return jax.ShapeDtypeStruct((4, rows, 128), F32)


def deal(blocks, keep_ref, cross_ref):
    me = lax.axis_index("gy")
    for sx in range(4):
        keep_ref[sx] = blocks[me ^ (2 * sx)]
        cross_ref[sx] = blocks[me ^ (2 * sx + 1)]


def arrived(refs):
    keep, cross, *far = refs
    return [keep.at[0], cross.at[0]] + [ref.at[i] for ref in far for i in range(2)]


def collect(parts, blocks):
    me = lax.axis_index("gy")
    for s in range(8):
        blocks[me ^ s] = parts[s][...]


def planes_kernel(got_ref, xl_ref, cy_hbm, keep_ref, cross_ref, cy_ref, planes, blocks, sem):
    copy = pltpu.make_async_copy(cy_hbm, cy_ref, sem)
    copy.start()
    transform_x(got_ref, xl_ref, planes)
    copy.wait()
    transform_y(planes, cy_ref, blocks)
    deal(blocks, keep_ref, cross_ref)


def planes(got, k):
    vmem = pl.BlockSpec(memory_space=pltpu.VMEM)
    return pl.pallas_call(
        planes_kernel,
        in_specs=[vmem, vmem, ANY],
        out_shape=[group_shape(72)] * 2,
        scratch_shapes=[
            pltpu.VMEM((8, 3, 16, 128), F32),
            pltpu.VMEM((8, 144, 128), F32),
            pltpu.VMEM((8, 72, 128), F32),
            pltpu.SemaphoreType.DMA,
        ],
        compiler_params=params(16),
        cost_estimate=cost(10**9, 3 * 10**6),
        name="planes",
    )(got, k["xl"], *in_hbm(k["cy"]))


def pair_up_kernel(keep_ref, cross_ref, *outs):
    for sx in range(1, 4):
        outs[sx - 1][0] = keep_ref[sx]
        outs[sx - 1][1] = cross_ref[sx]


def pair_up(keep, cross):
    shape = jax.ShapeDtypeStruct((2, *keep.shape[1:]), F32)
    return pl.pallas_call(
        pair_up_kernel,
        out_shape=[shape] * 3,
        compiler_params=params(16),
        cost_estimate=cost(10**6, 10**6),
        name="pair_up",
    )(keep, cross)


def exchange_second(blocks):
    keep, cross = blocks
    cross = across(cross, 1)
    pairs = pair_up(keep, cross)
    return [keep, cross] + [across(pair, 2 * sx + 2) for sx, pair in enumerate(pairs)]


def mode_grad_kernel(*refs):
    parts, (spread_ref, weight_hbm, gather_hbm, out_ref, grads_ref) = arrived(refs[:5]), refs[5:10]
    products, weight_ref, gather_ref, sems = refs[10:]
    copies = []
    for ky in range(3):
        copies.append(pltpu.make_async_copy(weight_hbm.at[ky], weight_ref.at[ky], sems.at[ky]))
    copies.append(pltpu.make_async_copy(gather_hbm, gather_ref, sems.at[3]))
    for copy in copies:
        copy.start()
    collect(parts, grads_ref)
    field = grads_ref[...].reshape(576, 128).astype(BF16)
    lanes = [dot(field, spread_ref[ky]) for ky in range(3)]
    total = None
    for j in range(4):
        if j < 3:
            copies[j].wait()
        for b in range(2):
            for t in range(3):
                ky, q = mode_of(j, t)
                for slot in range(3):
                    at = (3 * b + t) * 72 + slot * KS
                    source = (4 * b + q) * 72 + slot * KS
                    weight = weight_ref[ky, slot * 4 + q].astype(F32)
                    copy = lanes[ky][source : source + KS]
                    products[at : at + KS, :] = weight * jnp.concatenate([copy] * 8, axis=1)
        if j == 0:
            copies[3].wait()
        term = dot(products[...].astype(BF16), gather_ref[j])
        total = term if total is None else total + term
    out_ref[...] = total.reshape(TILES)


def mode_grad(parts, weights, k):
    vmem = pl.BlockSpec(memory_space=pltpu.VMEM)
    return pl.pallas_call(
        mode_grad_kernel,
        in_specs=[vmem] * 6 + [ANY] * 2,
        out_shape=[jax.ShapeDtypeStruct(TILES, F32), jax.ShapeDtypeStruct((8, 72, 128), F32)],
        scratch_shapes=[
            pltpu.VMEM((432, C * C), F32),
            pltpu.VMEM(weights.shape, BF16),
            pltpu.VMEM((4, C * C, 128), BF16),
            pltpu.SemaphoreType.DMA((4,)),
        ],
        compiler_params=params(16),
        cost_estimate=cost(10**9, 4 * 10**6),
        name="mode_grad",
    )(*parts, k["spread"], *in_hbm(weights, k["gather"]))


def backward_kernel(*refs):
    parts, (xl_ref, yb_hbm, sent_ref, yb_ref, blocks, sem) = refs[:8], refs[8:]
    me = lax.axis_index("gy")
    copy = pltpu.make_async_copy(yb_hbm.at[me], yb_ref, sem)
    copy.start()
    for s in range(8):
        blocks[me ^ s] = parts[s][...]
    group = lane_group(72)
    columns = []
    for s in range(8):
        tiles = []
        for b in range(2):
            three = [blocks[s, 3 * b + t] for t in range(3)]
            last = pltpu.roll(three[0], 32, 1)
            for t in range(1, 3):
                last = jnp.where(group == t, pltpu.roll(three[t], 32 + 32 * t, 1), last)
            tiles += three + [last]
        columns.append(jnp.concatenate(tiles, axis=0).astype(BF16))
    copy.wait()
    wide = dot_t(jnp.concatenate(columns, axis=1), yb_ref[...]).astype(BF16)
    for slot in range(3):
        both = []
        for d in range(8):
            rows = wide[d * 72 + slot * KS : d * 72 + slot * KS + KS]
            both.append(jnp.concatenate([rows[:, :128], rows[:, 128:]], axis=0))
        both = jnp.concatenate(both, axis=1)
        out = dot(xl_ref[...], jnp.concatenate([both, both], axis=0))
        for d in range(8):
            sent_ref[:, d, slot] = out[:, d * 128 : d * 128 + 128].reshape(16, 8, 128)


def backward(parts, k):
    vmem = pl.BlockSpec(memory_space=pltpu.VMEM)
    return pl.pallas_call(
        backward_kernel,
        in_specs=[vmem] * 9 + [ANY],
        out_shape=pltpu.HBM(SENT_SHAPE, F32),
        out_specs=pl.BlockSpec(SENT_SHAPE, lambda: (0,) * 5),
        scratch_shapes=[
            pltpu.VMEM((256, 1024), BF16),
            pltpu.VMEM((8, *TILES), F32),
            pltpu.SemaphoreType.DMA,
        ],
        compiler_params=params(16),
        cost_estimate=cost(10**9, 4 * 10**6),
        name="backward",
    )(*parts, k["xl_t"], *in_hbm(k["yb"]))


def spectral_grad_kernel(grads_ref, *refs):
    fields, (spread_ref, wide_ref, out_ref) = refs[:4], refs[4:]
    ky = pl.program_id(0)

    def tile(t):
        value = fields[0][t] + fields[1][t] + fields[2][t] + fields[3][t]
        return value.astype(BF16)

    copies = dot(grads_ref[...].reshape(576, 128).astype(BF16), spread_ref[ky])
    for q in range(4):
        j, t = (ky, q) if q < 3 else (3, ky)
        field = jnp.concatenate([tile(t), tile(3 + t)], axis=0)
        wide = dot(field, wide_ref[j])
        for slot in range(3):
            total = None
            for b in range(2):
                at = b * 72 + slot * KS
                source = (4 * b + q) * 72 + slot * KS
                copy = copies[source : source + KS]
                term = wide[at : at + KS] * jnp.concatenate([copy] * 8, axis=1)
                total = term if total is None else total + term
            out_ref[0, slot * 4 + q] = total


def spectral_grad(grads, fields, k):
    return pl.pallas_call(
        spectral_grad_kernel,
        grid=(3,),
        in_specs=[whole((8, 72, 128))]
        + [whole(TILES)] * 4
        + [whole((4, 128, 128)), whole((4, 128, C * C))],
        out_specs=pl.BlockSpec((1, 12, KS, C * C), lambda i: (i, 0, 0, 0)),
        out_shape=pltpu.HBM((3, 12, KS, C * C), F32),
        compiler_params=params(24),
        cost_estimate=cost(10**9, 4 * 10**6),
        name="spectral_grad",
    )(grads, *fields, *in_hbm(k["spread"], k["wide"]))


def synthesise_kernel(got_ref, grad_ref, table_ref, zl_ref, mix_ref, out_ref, parts):
    step = pl.program_id(1)

    @pl.when(step == 0)
    def _():
        group = lane_group(8 * KS)
        for half in range(2):
            turned = []
            for q in range(4):
                tiles = []
                for kz in range(KS):
                    block, slot = divmod(2 * kz + half, 3)
                    tiles.append(got_ref[block, q, slot])
                value = jnp.concatenate(tiles, axis=0)
                turned.append(pltpu.roll(value, q * C, 1) if q else value)
            for p in range(4):
                value = turned[(-p) % 4]
                for g in range(1, 4):
                    value = jnp.where(group == g, turned[(g - p) % 4], value)
                parts[p, :, half * 128 : half * 128 + 128] = value.astype(BF16)

    for pair in range(2):
        timed = dot(parts[2 * step + pair], table_ref[pair]).astype(BF16)
        timed = jnp.concatenate([timed, jnp.zeros((64, NT * C), BF16)], axis=0)
        ys = slice(2 * pair, 2 * pair + 2)
        grad = grad_ref[0, :, ys].reshape(8 * N, NT * C)
        for side in range(2):
            lanes = slice(side * 256, side * 256 + 256)
            left = jnp.concatenate([zl_ref[...], grad[:, lanes]], axis=1)
            right = jnp.concatenate([timed[:, lanes], mix_ref[...]], axis=0)
            out_ref[0, :, ys, :, lanes] = dot(left, right).astype(BF16).reshape(4, 2, N, 256)


def synthesise(got, grad, mix, k):
    return pl.pallas_call(
        synthesise_kernel,
        grid=(2, 2),
        in_specs=[SENT, FIELD, TABLE_T, whole((8 * N, 256)), whole((256, 256))],
        out_specs=FIELD,
        out_shape=pltpu.HBM(grad.shape, BF16),
        scratch_shapes=[pltpu.VMEM((4, 8 * KS, MT * C), BF16)],
        compiler_params=params(24),
        cost_estimate=cost(4 * 10**9, 10 * 10**6),
        name="synthesise",
    )(got, *in_hbm(grad, k["tables_t"], k["zl_t"], mix))


def exchange_all(block):
    flat = block.reshape(128, 24, 128)
    return lax.all_to_all(flat, ("gx", "gy"), 0, 0, tiled=True).reshape(block.shape)


def exchange_first(block):
    flat = block.reshape(16, 192, 128)
    return lax.all_to_all(flat, "gx", 0, 0, tiled=True).reshape(block.shape)


def body(inputs, cotangent, pre_activation, pointwise, spectral):
    k = constants()
    weights = jnp.transpose(spectral, (1, 2, 0, 3))
    mix = jnp.kron(jnp.eye(8, dtype=BF16), pointwise.T)
    sent, grad_pre = analyse_grad(cotangent, pre_activation, k)
    got = exchange_all(sent)
    sent_input = analyse_input(inputs, k)
    got, *_ = lax.optimization_barrier((got, sent_input, mix))
    got_input = exchange_first(sent_input)
    modes, grads = mode_grad(exchange_second(planes(got, k)), weights, k)
    parts = gather_second(modes)
    got_input, *_ = lax.optimization_barrier((got_input, modes))
    sums = reduce_cores(forward(got_input, k))
    back = exchange_first(backward(parts, k))
    weight_grad = spectral_grad(grads, reduce_chips(sums), k)
    return synthesise(back, grad_pre, mix, k), jnp.transpose(weight_grad, (2, 0, 1, 3))


def solution(mesh):
    in_specs = (
        P(None, "gx", "gy", None, None),
        P(None, "gx", "gy", None, None),
        P(None, "gx", "gy", None, None),
        P(),
        P(None, "gy", "gx", None),
    )
    out_specs = (P(None, "gx", "gy", None, None), P(None, "gy", "gx", None))
    return jax.shard_map(body, mesh=mesh, in_specs=in_specs, out_specs=out_specs, check_vma=False)
```

```python
import functools
import math

import jax
import jax.numpy as jnp
import ml_dtypes
import numpy as np
from jax import lax
from jax.experimental import pallas as pl
from jax.experimental.pallas import tpu as pltpu
from jax.sharding import PartitionSpec as P

N = 64
NT = 16
MS = 12
MT = 8
KS = 24
C = 32
BF = ml_dtypes.bfloat16
F32 = jnp.float32
BF16 = jnp.bfloat16
MIB = 1 << 20


def fourier(length, frequencies):
    points = np.arange(length, dtype=np.float64)[:, None]
    orders = np.arange(frequencies, dtype=np.float64)[None, :]
    scales = np.where(orders == 0.0, math.sqrt(1.0 / length), math.sqrt(2.0 / length))
    cosines = scales * np.cos(2.0 * math.pi * points * orders / length)
    sines = math.sqrt(2.0 / length) * np.sin(2.0 * math.pi * points * (orders + 1.0) / length)
    return np.concatenate([cosines, sines], axis=1).astype(np.float32)


def cosine(length, modes):
    points = np.arange(length, dtype=np.float64)[:, None]
    orders = np.arange(modes, dtype=np.float64)[None, :]
    scales = np.where(orders == 0.0, math.sqrt(1.0 / length), math.sqrt(2.0 / length))
    return (scales * np.cos(math.pi * orders * (points + 0.5) / length)).astype(np.float32)


def constants():
    basis = fourier(N, MS)
    third = basis.astype(BF).astype(np.float32)
    time = cosine(NT, MT).astype(BF).astype(np.float32)
    eye_c = np.eye(C, dtype=np.float32)
    eye_r = np.eye(8, dtype=np.float32)
    out = {}
    tables = np.zeros((4, NT, C, 2, 4, C), np.float32)
    for pair in range(4):
        for kt in range(MT):
            half, q = divmod(kt, 4)
            tables[pair, :, :, half, (q + pair) % 4, :] = time[:, kt][:, None, None] * eye_c[None]
    tables = tables.reshape(4, NT * C, MT * C)
    out["tables"] = tables.astype(BF)
    out["tables_t"] = np.swapaxes(tables, 1, 2).copy().astype(BF)
    zl = np.einsum("zk,rs->krsz", third, eye_r).reshape(KS * 8, 8 * N)
    out["zl"] = zl.astype(BF)
    out["zl_t"] = zl.T.copy().astype(BF)
    high = basis.astype(BF).astype(np.float32)
    low = (basis - high).astype(BF).astype(np.float32)
    eye_h = np.eye(2, dtype=np.float32)
    forms = [np.einsum("xk,hg->hkxg", part, eye_h).reshape(2 * KS, 2 * N) for part in (high, low)]
    out["xl"] = np.concatenate(forms, axis=1).astype(BF)
    out["xl_t"] = np.concatenate([form.T for form in forms], axis=1).astype(BF)
    padded = np.zeros((N, 8, 4), np.float32)
    padded[:, :, :3] = basis.reshape(N, 8, 3)
    yb = np.einsum("slhdk,ce->shlcdke", padded.reshape(8, 4, 2, 8, 4), eye_c)
    out["yb"] = yb.reshape(8, 256, 1024).astype(BF)
    second = basis.reshape(8, 4, 2, 8, 3)
    out["cy"] = np.repeat(np.einsum("slhdj->djhsl", second).reshape(8, 3, 16, 4), C, axis=3)
    spread = np.zeros((4, 4, C, 4, C), np.float32)
    gather = np.zeros((4, C, C, 4, C), np.float32)
    wide = np.zeros((4, 4, C, C, C), np.float32)
    for j in range(4):
        spread[j, j] = eye_c[:, None, :]
        gather[j, :, :, j, :] = eye_c[:, None, :]
        wide[j, j] = eye_c[:, :, None]
    out["spread"] = spread.reshape(4, 128, 128).astype(BF)
    out["gather"] = gather.reshape(4, C * C, 128).astype(BF)
    out["wide"] = wide.reshape(4, 128, C * C).astype(BF)
    return out


def dot(a, b):
    return jnp.dot(a, b, preferred_element_type=F32)


def dot_t(a, b):
    return lax.dot_general(a, b, (((1,), (1,)), ((), ())), preferred_element_type=F32)


def gelu_slope(v):
    cdf = 0.5 * (1.0 + lax.erf(v * 0.7071067811865476))
    return cdf + v * (0.3989422804014327 * jnp.exp(-0.5 * v * v))


def lane_group(rows):
    return lax.broadcasted_iota(jnp.int32, (rows, 128), 1) // C


def send_parts(parts, sent_ref):
    group = lane_group(8 * KS)
    for half in range(2):
        lanes = slice(half * 128, half * 128 + 128)
        for q in range(4):
            value = parts[(-q) % 4, :, lanes]
            for p in range(1, 4):
                value = jnp.where(group == p, parts[(p - q) % 4, :, lanes], value)
            if q:
                value = pltpu.roll(value, 128 - q * C, 1)
            for kz in range(KS):
                block, slot = divmod(2 * kz + half, 3)
                sent_ref[block, q, slot] = value[kz * 8 : kz * 8 + 8]


def analyse_grad_kernel(cot_ref, pre_ref, table_ref, zl_ref, sent_ref, even, odd, parts):
    step = pl.program_id(1)

    def cells(pair, flat):
        for x in range(4):
            for y in range(2):
                for j in range(4):
                    rows = slice(j * 16, j * 16 + 16)
                    v = pre_ref[0, x, 2 * pair + y, rows, :].astype(F32)
                    g = cot_ref[0, x, 2 * pair + y, rows, :].astype(F32)
                    at = (2 * x + y) * N + j * 16
                    flat[at : at + 16, :] = (g * gelu_slope(v)).astype(BF16)

    def analyse(pair, flat):
        sectioned = dot(zl_ref[...], flat[...]).astype(BF16)
        parts[pair] = dot(sectioned, table_ref[pair])

    analyse((2 * step + 3) % 4, odd)
    cells(0, even)
    analyse(2 * step, even)
    cells(1, odd)

    @pl.when(step == 1)
    def _():
        analyse(3, odd)
        send_parts(parts, sent_ref)


def analyse_input_kernel(field_ref, table_ref, zl_ref, weight_ref, sent_ref, mix_ref, parts):
    step = pl.program_id(1)

    @pl.when((step == 0) & (pl.program_id(0) == 0))
    def _():
        rows = lax.broadcasted_iota(jnp.int32, (256, C), 0) % C
        copies = (rows == lax.broadcasted_iota(jnp.int32, (256, C), 1)).astype(BF16)
        mixed = dot_t(dot_t(copies, weight_ref[...]).astype(BF16), copies)
        blocks = [lax.broadcasted_iota(jnp.int32, (256, 256), axis) // C for axis in range(2)]
        mix_ref[...] = jnp.where(blocks[0] == blocks[1], mixed, 0.0).astype(BF16)
    for pair in range(2):
        field = field_ref[0, :, 2 * pair : 2 * pair + 2].reshape(8 * N, NT * C)
        sectioned = dot(zl_ref[...], field).astype(BF16)
        parts[2 * step + pair] = dot(sectioned, table_ref[pair])

    @pl.when(step == 1)
    def _():
        send_parts(parts, sent_ref)


FIELD = pl.BlockSpec((1, 4, 4, N, NT * C), lambda b, p: (b, 0, p, 0, 0))
TABLE = pl.BlockSpec((2, NT * C, MT * C), lambda b, p: (p, 0, 0))
TABLE_T = pl.BlockSpec((2, MT * C, NT * C), lambda b, p: (p, 0, 0))
SENT = pl.BlockSpec((16, 4, 3, 8, 128), lambda b, p: (0, b, 0, 0, 0))
SENT_SHAPE = (16, 8, 3, 8, 128)
TILES = (6, 72, 128)
ANY = pl.BlockSpec(memory_space=pl.ANY)


def whole(shape):
    return pl.BlockSpec(shape, lambda *ids: (0,) * len(shape))


def params(limit):
    return pltpu.CompilerParams(vmem_limit_bytes=limit * MIB)


def cost(flops, nbytes):
    return pl.CostEstimate(flops=flops, bytes_accessed=nbytes, transcendentals=0)


def in_hbm(*arrays):
    return [pltpu.with_memory_space_constraint(a, pltpu.HBM) for a in arrays]


def analyse_grad(cotangent, pre_activation, k):
    return pl.pallas_call(
        analyse_grad_kernel,
        grid=(2, 2),
        in_specs=[FIELD, FIELD, whole((4, NT * C, MT * C)), whole((8 * KS, 8 * N))],
        out_specs=SENT,
        out_shape=pltpu.HBM(SENT_SHAPE, F32),
        scratch_shapes=[
            pltpu.VMEM((8 * N, NT * C), BF16),
            pltpu.VMEM((8 * N, NT * C), BF16),
            pltpu.VMEM((4, 8 * KS, MT * C), F32),
        ],
        compiler_params=params(24),
        cost_estimate=cost(4 * 10**9, 14 * 10**6),
        name="analyse_grad",
    )(*in_hbm(cotangent, pre_activation, k["tables"], k["zl"]))


def mix_channels_kernel(cot_ref, pre_ref, mix_ref, out_ref, even, odd):
    def cells(pair, flat):
        for x in range(4):
            for y in range(2):
                for j in range(4):
                    rows = slice(j * 16, j * 16 + 16)
                    v = pre_ref[0, x, 2 * pair + y, rows, :].astype(F32)
                    g = cot_ref[0, x, 2 * pair + y, rows, :].astype(F32)
                    at = (2 * x + y) * N + j * 16
                    flat[at : at + 16, :] = (g * gelu_slope(v)).astype(BF16)

    def mix(pair, flat):
        for side in range(2):
            lanes = slice(side * 256, side * 256 + 256)
            mixed = dot(flat[:, lanes], mix_ref[...]).astype(BF16)
            out_ref[0, :, 2 * pair : 2 * pair + 2, :, lanes] = mixed.reshape(4, 2, N, 256)

    cells(0, even)
    mix(0, even)
    cells(1, odd)
    mix(1, odd)


def mix_channels(cotangent, pre_activation, mix):
    return pl.pallas_call(
        mix_channels_kernel,
        grid=(2, 2),
        in_specs=[FIELD, FIELD, whole((256, 256))],
        out_specs=FIELD,
        out_shape=pltpu.HBM(cotangent.shape, BF16),
        scratch_shapes=[pltpu.VMEM((8 * N, NT * C), BF16)] * 2,
        compiler_params=params(24),
        cost_estimate=cost(4 * 10**9, 12 * 10**6),
        name="mix_channels",
    )(*in_hbm(cotangent, pre_activation, mix))


def analyse_input(inputs, pointwise, k):
    return pl.pallas_call(
        analyse_input_kernel,
        grid=(2, 2),
        in_specs=[FIELD, TABLE, whole((8 * KS, 8 * N)), whole((C, C))],
        out_specs=[SENT, whole((256, 256))],
        out_shape=[pltpu.HBM(SENT_SHAPE, F32), pltpu.HBM((256, 256), BF16)],
        scratch_shapes=[pltpu.VMEM((4, 8 * KS, MT * C), F32)],
        compiler_params=params(24),
        cost_estimate=cost(4 * 10**9, 6 * 10**6),
        name="analyse_input",
    )(*in_hbm(inputs, k["tables"], k["zl"], pointwise))


def mode_of(j, t):
    return (j, t) if j < 3 else (t, 3)


def forward_kernel(got_ref, xl_ref, yb_hbm, keep_ref, cross_ref, yb_ref, fields, blocks, sem):
    me = lax.axis_index("gy")
    copy = pltpu.make_async_copy(yb_hbm.at[me], yb_ref, sem)
    copy.start()
    for slot in range(3):
        field = jnp.concatenate(
            [got_ref[:, d, slot].reshape(128, 128).astype(BF16) for d in range(8)], axis=1
        )
        wide = dot(xl_ref[...], jnp.concatenate([field, field], axis=0))
        for d in range(8):
            for half in range(2):
                rows = slice(d * 72 + slot * KS, d * 72 + slot * KS + KS)
                fields[rows, half * 128 : half * 128 + 128] = wide[
                    half * KS : half * KS + KS, d * 128 : d * 128 + 128
                ]
    copy.wait()
    group = lane_group(72)
    field = fields[...].astype(BF16)
    for to in range(8):
        part = dot(field, yb_ref[:, to * 128 : to * 128 + 128])
        for b in range(2):
            last = part[(4 * b + 3) * 72 : (4 * b + 4) * 72]
            for t in range(3):
                value = part[(4 * b + t) * 72 : (4 * b + t + 1) * 72]
                blocks[to, 3 * b + t] = jnp.where(group == 3, pltpu.roll(last, 96 - 32 * t, 1), value)
    for sx in range(4):
        keep_ref[sx] = blocks[me ^ (2 * sx)]
        cross_ref[sx] = blocks[me ^ (2 * sx + 1)]


def forward(got, k):
    vmem = pl.BlockSpec(memory_space=pltpu.VMEM)
    return pl.pallas_call(
        forward_kernel,
        in_specs=[vmem, vmem, ANY],
        out_shape=[jax.ShapeDtypeStruct((4, *TILES), F32)] * 2,
        scratch_shapes=[
            pltpu.VMEM((256, 1024), BF16),
            pltpu.VMEM((576, 256), F32),
            pltpu.VMEM((8, *TILES), F32),
            pltpu.SemaphoreType.DMA,
        ],
        compiler_params=params(16),
        cost_estimate=cost(10**9, 4 * 10**6),
        name="forward",
    )(got, k["xl"], *in_hbm(k["yb"]))


def add_cores_kernel(keep_ref, cross_ref, *outs):
    for sx in range(4):
        outs[sx][...] = keep_ref[sx] + cross_ref[sx]


def add_cores(keep, cross):
    return pl.pallas_call(
        add_cores_kernel,
        out_shape=[jax.ShapeDtypeStruct(TILES, F32)] * 4,
        compiler_params=params(16),
        cost_estimate=cost(10**6, 10**6),
        name="add_cores",
    )(keep, cross)


def across(block, sx):
    return lax.ppermute(block, "gy", [(i, i ^ sx) for i in range(8)])


def reduce_cores(blocks):
    keep, cross = blocks
    return add_cores(keep, across(cross, 1))


def reduce_chips(sums):
    own, *others = sums
    return [own] + [across(other, 2 * sx + 2) for sx, other in enumerate(others)]


def gather_second(block):
    parts = [block, across(block, 1)]
    for sx in range(1, 4):
        far = across(block, 2 * sx)
        parts += [far, across(far, 1)]
    return parts


def transform_x(got_ref, xl_ref, planes):
    for slot in range(3):
        field = jnp.concatenate(
            [got_ref[:, s, slot].reshape(128, 128).astype(BF16) for s in range(8)], axis=1
        )
        wide = dot(xl_ref[...], jnp.concatenate([field, field], axis=0))
        for s in range(8):
            planes[s, slot * 48 : slot * 48 + 48, :] = wide[:, s * 128 : s * 128 + 128]


def transform_y(planes, cy_ref, blocks):
    group = lane_group(72)

    def block(d, carry):
        totals = [jnp.zeros((72, 128), F32)] * 3
        for s in range(8):
            for half in range(2):
                starts = [slot * 48 + half * KS for slot in range(3)]
                rows = jnp.concatenate([planes[s, at : at + KS, :] for at in starts], axis=0)
                for j in range(3):
                    totals[j] = totals[j] + rows * cy_ref[d, j, half * 8 + s : half * 8 + s + 1, :]
        value = jnp.zeros((72, 128), F32)
        for j in range(3):
            total = totals[j] + pltpu.roll(totals[j], 64, 1)
            total = total + pltpu.roll(total, 32, 1)
            value = jnp.where(group == j, total, value)
        blocks[d] = value
        return carry

    lax.fori_loop(0, 8, block, 0)


def group_shape(rows):
    return jax.ShapeDtypeStruct((4, rows, 128), F32)


def deal(blocks, keep_ref, cross_ref):
    me = lax.axis_index("gy")
    for sx in range(4):
        keep_ref[sx] = blocks[me ^ (2 * sx)]
        cross_ref[sx] = blocks[me ^ (2 * sx + 1)]


def arrived(refs):
    keep, cross, *far = refs
    return [keep.at[0], cross.at[0]] + [ref.at[i] for ref in far for i in range(2)]


def collect(parts, blocks):
    me = lax.axis_index("gy")
    for s in range(8):
        blocks[me ^ s] = parts[s][...]


def planes_kernel(got_ref, xl_ref, cy_hbm, keep_ref, cross_ref, cy_ref, planes, blocks, sem):
    copy = pltpu.make_async_copy(cy_hbm, cy_ref, sem)
    copy.start()
    transform_x(got_ref, xl_ref, planes)
    copy.wait()
    transform_y(planes, cy_ref, blocks)
    deal(blocks, keep_ref, cross_ref)


def planes(got, k):
    vmem = pl.BlockSpec(memory_space=pltpu.VMEM)
    return pl.pallas_call(
        planes_kernel,
        in_specs=[vmem, vmem, ANY],
        out_shape=[group_shape(72)] * 2,
        scratch_shapes=[
            pltpu.VMEM((8, 3, 16, 128), F32),
            pltpu.VMEM((8, 144, 128), F32),
            pltpu.VMEM((8, 72, 128), F32),
            pltpu.SemaphoreType.DMA,
        ],
        compiler_params=params(16),
        cost_estimate=cost(10**9, 3 * 10**6),
        name="planes",
    )(got, k["xl"], *in_hbm(k["cy"]))


def pair_up_kernel(keep_ref, cross_ref, *outs):
    for sx in range(1, 4):
        outs[sx - 1][0] = keep_ref[sx]
        outs[sx - 1][1] = cross_ref[sx]


def pair_up(keep, cross):
    shape = jax.ShapeDtypeStruct((2, *keep.shape[1:]), F32)
    return pl.pallas_call(
        pair_up_kernel,
        out_shape=[shape] * 3,
        compiler_params=params(16),
        cost_estimate=cost(10**6, 10**6),
        name="pair_up",
    )(keep, cross)


def exchange_second(blocks):
    keep, cross = blocks
    cross = across(cross, 1)
    pairs = pair_up(keep, cross)
    return [keep, cross] + [across(pair, 2 * sx + 2) for sx, pair in enumerate(pairs)]


def mode_grad_kernel(*refs):
    parts, (spread_ref, weight_hbm, gather_hbm, out_ref, grads_ref) = arrived(refs[:5]), refs[5:10]
    weight_ref, gather_ref, sems = refs[10:]
    copies = []
    for ky in range(3):
        copies.append(pltpu.make_async_copy(weight_hbm.at[ky], weight_ref.at[ky], sems.at[0, ky]))
        copies.append(pltpu.make_async_copy(gather_hbm.at[ky], gather_ref.at[ky], sems.at[1, ky]))
    for copy in copies:
        copy.start()
    collect(parts, grads_ref)
    field = []
    for b in range(2):
        for slot in range(3):
            for q in range(4):
                field.append(grads_ref[4 * b + q, slot * KS : slot * KS + KS, :])
    field = jnp.concatenate(field, axis=0).astype(BF16)
    total = None
    for ky in range(3):
        lanes = dot(field, spread_ref[ky]).astype(BF16)
        copies[2 * ky].wait()
        products = []
        for b in range(2):
            copy = lanes[b * 288 : b * 288 + 288]
            products.append(weight_ref[ky] * jnp.concatenate([copy] * 8, axis=1))
        copies[2 * ky + 1].wait()
        term = dot(jnp.concatenate(products, axis=0), gather_ref[ky])
        total = term if total is None else total + term
    group = lane_group(72)
    for b in range(2):
        modes = []
        for q in range(4):
            starts = [b * 288 + (slot * 4 + q) * KS for slot in range(3)]
            modes.append(jnp.concatenate([total[at : at + KS] for at in starts], axis=0))
        for t in range(3):
            out_ref[3 * b + t] = jnp.where(group == 3, pltpu.roll(modes[3], 96 - 32 * t, 1), modes[t])


def mode_grad(parts, weights, k):
    vmem = pl.BlockSpec(memory_space=pltpu.VMEM)
    return pl.pallas_call(
        mode_grad_kernel,
        in_specs=[vmem] * 6 + [ANY] * 2,
        out_shape=[jax.ShapeDtypeStruct(TILES, F32), jax.ShapeDtypeStruct((8, 72, 128), F32)],
        scratch_shapes=[
            pltpu.VMEM((3, 12 * KS, C * C), BF16),
            pltpu.VMEM((4, C * C, 128), BF16),
            pltpu.SemaphoreType.DMA((2, 3)),
        ],
        compiler_params=params(16),
        cost_estimate=cost(10**9, 4 * 10**6),
        name="mode_grad",
    )(*parts, k["spread"], *in_hbm(weights.reshape(3, 12 * KS, C * C), k["gather"]))


def backward_kernel(*refs):
    parts, (xl_ref, yb_hbm, sent_ref, yb_ref, blocks, sem) = refs[:8], refs[8:]
    me = lax.axis_index("gy")
    copy = pltpu.make_async_copy(yb_hbm.at[me], yb_ref, sem)
    copy.start()
    for s in range(8):
        blocks[me ^ s] = parts[s][...]
    group = lane_group(72)
    columns = []
    for s in range(8):
        tiles = []
        for b in range(2):
            three = [blocks[s, 3 * b + t] for t in range(3)]
            last = pltpu.roll(three[0], 32, 1)
            for t in range(1, 3):
                last = jnp.where(group == t, pltpu.roll(three[t], 32 + 32 * t, 1), last)
            tiles += three + [last]
        columns.append(jnp.concatenate(tiles, axis=0).astype(BF16))
    copy.wait()
    wide = dot_t(jnp.concatenate(columns, axis=1), yb_ref[...]).astype(BF16)
    for slot in range(3):
        both = []
        for d in range(8):
            rows = wide[d * 72 + slot * KS : d * 72 + slot * KS + KS]
            both.append(jnp.concatenate([rows[:, :128], rows[:, 128:]], axis=0))
        both = jnp.concatenate(both, axis=1)
        out = dot(xl_ref[...], jnp.concatenate([both, both], axis=0))
        for d in range(8):
            sent_ref[:, d, slot] = out[:, d * 128 : d * 128 + 128].reshape(16, 8, 128)


def backward(parts, k):
    vmem = pl.BlockSpec(memory_space=pltpu.VMEM)
    return pl.pallas_call(
        backward_kernel,
        in_specs=[vmem] * 9 + [ANY],
        out_shape=pltpu.HBM(SENT_SHAPE, F32),
        out_specs=pl.BlockSpec(SENT_SHAPE, lambda: (0,) * 5),
        scratch_shapes=[
            pltpu.VMEM((256, 1024), BF16),
            pltpu.VMEM((8, *TILES), F32),
            pltpu.SemaphoreType.DMA,
        ],
        compiler_params=params(16),
        cost_estimate=cost(10**9, 4 * 10**6),
        name="backward",
    )(*parts, k["xl_t"], *in_hbm(k["yb"]))


def spectral_grad_kernel(grads_ref, *refs):
    fields, (spread_ref, wide_ref, out_ref) = refs[:4], refs[4:]
    ky = pl.program_id(0)

    def tile(t):
        value = fields[0][t] + fields[1][t] + fields[2][t] + fields[3][t]
        return value.astype(BF16)

    copies = dot(grads_ref[...].reshape(576, 128).astype(BF16), spread_ref[ky])
    for q in range(4):
        j, t = (ky, q) if q < 3 else (3, ky)
        field = jnp.concatenate([tile(t), tile(3 + t)], axis=0)
        wide = dot(field, wide_ref[j])
        for slot in range(3):
            total = None
            for b in range(2):
                at = b * 72 + slot * KS
                source = (4 * b + q) * 72 + slot * KS
                copy = copies[source : source + KS]
                term = wide[at : at + KS] * jnp.concatenate([copy] * 8, axis=1)
                total = term if total is None else total + term
            out_ref[0, slot * 4 + q] = total


def spectral_grad(grads, fields, k):
    return pl.pallas_call(
        spectral_grad_kernel,
        grid=(3,),
        in_specs=[whole((8, 72, 128))]
        + [whole(TILES)] * 4
        + [whole((4, 128, 128)), whole((4, 128, C * C))],
        out_specs=pl.BlockSpec((1, 12, KS, C * C), lambda i: (i, 0, 0, 0)),
        out_shape=pltpu.HBM((3, 12, KS, C * C), F32),
        compiler_params=params(24),
        cost_estimate=cost(10**9, 4 * 10**6),
        name="spectral_grad",
    )(grads, *fields, *in_hbm(k["spread"], k["wide"]))


def synthesise_kernel(got_ref, mixed_ref, table_ref, zl_ref, out_ref, parts):
    step = pl.program_id(1)

    @pl.when(step == 0)
    def _():
        group = lane_group(8 * KS)
        for half in range(2):
            turned = []
            for q in range(4):
                tiles = []
                for kz in range(KS):
                    block, slot = divmod(2 * kz + half, 3)
                    tiles.append(got_ref[block, q, slot])
                value = jnp.concatenate(tiles, axis=0)
                turned.append(pltpu.roll(value, q * C, 1) if q else value)
            for p in range(4):
                value = turned[(-p) % 4]
                for g in range(1, 4):
                    value = jnp.where(group == g, turned[(g - p) % 4], value)
                parts[p, :, half * 128 : half * 128 + 128] = value.astype(BF16)

    for pair in range(2):
        timed = dot(parts[2 * step + pair], table_ref[pair]).astype(BF16)
        ys = slice(2 * pair, 2 * pair + 2)
        value = dot(zl_ref[...], timed).reshape(4, 2, N, NT * C)
        out_ref[0, :, ys] = (value + mixed_ref[0, :, ys].astype(F32)).astype(BF16)


def synthesise(got, mixed, k):
    return pl.pallas_call(
        synthesise_kernel,
        grid=(2, 2),
        in_specs=[SENT, FIELD, TABLE_T, whole((8 * N, 8 * KS))],
        out_specs=FIELD,
        out_shape=pltpu.HBM(mixed.shape, BF16),
        scratch_shapes=[pltpu.VMEM((4, 8 * KS, MT * C), BF16)],
        compiler_params=params(24),
        cost_estimate=cost(4 * 10**9, 10 * 10**6),
        name="synthesise",
    )(got, *in_hbm(mixed, k["tables_t"], k["zl_t"]))


def exchange_all(block):
    flat = block.reshape(128, 24, 128)
    return lax.all_to_all(flat, ("gx", "gy"), 0, 0, tiled=True).reshape(block.shape)


def exchange_first(block):
    flat = block.reshape(16, 192, 128)
    return lax.all_to_all(flat, "gx", 0, 0, tiled=True).reshape(block.shape)


def body(inputs, cotangent, pre_activation, pointwise, spectral):
    k = constants()
    weights = jnp.transpose(spectral, (1, 2, 0, 3))
    sent = analyse_grad(cotangent, pre_activation, k)
    got = exchange_all(sent)
    sent_input, mix = analyse_input(inputs, pointwise, k)
    mixed = mix_channels(cotangent, pre_activation, mix)
    got, *_ = lax.optimization_barrier((got, sent_input, mixed))
    blocks = planes(got, k)
    sent_input, *_ = lax.optimization_barrier((sent_input, blocks[0]))
    got_input = exchange_first(sent_input)
    modes, grads = mode_grad(exchange_second(blocks), weights, k)
    got_input, *_ = lax.optimization_barrier((got_input, modes))
    sums = reduce_cores(forward(got_input, k))
    back = exchange_first(backward(gather_second(modes), k))
    weight_grad = spectral_grad(grads, reduce_chips(sums), k)
    back, *_ = lax.optimization_barrier((back, weight_grad))
    return synthesise(back, mixed, k), jnp.transpose(weight_grad, (2, 0, 1, 3))


def solution(mesh):
    in_specs = (
        P(None, "gx", "gy", None, None),
        P(None, "gx", "gy", None, None),
        P(None, "gx", "gy", None, None),
        P(),
        P(None, "gy", "gx", None),
    )
    out_specs = (P(None, "gx", "gy", None, None), P(None, "gy", "gx", None))
    return jax.shard_map(body, mesh=mesh, in_specs=in_specs, out_specs=out_specs, check_vma=False)
```

```python
import functools
import math

import jax
import jax.numpy as jnp
import ml_dtypes
import numpy as np
from jax import lax
from jax.experimental import pallas as pl
from jax.experimental.pallas import tpu as pltpu
from jax.sharding import PartitionSpec as P

N = 64
NT = 16
MS = 12
MT = 8
KS = 24
C = 32
BF = ml_dtypes.bfloat16
F32 = jnp.float32
BF16 = jnp.bfloat16
MIB = 1 << 20


def fourier(length, frequencies):
    points = np.arange(length, dtype=np.float64)[:, None]
    orders = np.arange(frequencies, dtype=np.float64)[None, :]
    scales = np.where(orders == 0.0, math.sqrt(1.0 / length), math.sqrt(2.0 / length))
    cosines = scales * np.cos(2.0 * math.pi * points * orders / length)
    sines = math.sqrt(2.0 / length) * np.sin(2.0 * math.pi * points * (orders + 1.0) / length)
    return np.concatenate([cosines, sines], axis=1).astype(np.float32)


def cosine(length, modes):
    points = np.arange(length, dtype=np.float64)[:, None]
    orders = np.arange(modes, dtype=np.float64)[None, :]
    scales = np.where(orders == 0.0, math.sqrt(1.0 / length), math.sqrt(2.0 / length))
    return (scales * np.cos(math.pi * orders * (points + 0.5) / length)).astype(np.float32)


def constants():
    basis = fourier(N, MS)
    third = basis.astype(BF).astype(np.float32)
    time = cosine(NT, MT).astype(BF).astype(np.float32)
    eye_c = np.eye(C, dtype=np.float32)
    eye_r = np.eye(8, dtype=np.float32)
    out = {}
    table = np.einsum("tm,cd->tcmd", time, eye_c).reshape(NT * C, MT * C)
    out["table"] = table.astype(BF)
    out["table_t"] = table.T.copy().astype(BF)
    zl = np.einsum("zk,rs->krsz", third, eye_r).reshape(KS * 8, 8 * N)
    out["zl"] = zl.astype(BF)
    out["zl_t"] = zl.T.copy().astype(BF)
    high = basis.astype(BF).astype(np.float32)
    low = (basis - high).astype(BF).astype(np.float32)
    eye_h = np.eye(2, dtype=np.float32)
    forms = [np.einsum("xk,hg->hkxg", part, eye_h).reshape(2 * KS, 2 * N) for part in (high, low)]
    out["xl"] = np.concatenate(forms, axis=1).astype(BF)
    out["xl_t"] = np.concatenate([form.T for form in forms], axis=1).astype(BF)
    padded = np.zeros((N, 8, 4), np.float32)
    padded[:, :, :3] = basis.reshape(N, 8, 3)
    yb = np.einsum("slhdk,ce->shlcdke", padded.reshape(8, 4, 2, 8, 4), eye_c)
    yb = yb.reshape(8, 256, 1024).astype(BF)
    out["yb"] = yb
    out["yb_t"] = np.swapaxes(yb, 1, 2).copy()
    second = basis.reshape(8, 4, 2, 8, 3)
    out["cy"] = np.repeat(np.einsum("slhdj->djhsl", second).reshape(8, 3, 16, 4), C, axis=3)
    spread = np.zeros((4, 4, C, 4, C), np.float32)
    gather = np.zeros((4, C, C, 4, C), np.float32)
    wide = np.zeros((4, 4, C, C, C), np.float32)
    for j in range(4):
        spread[j, j] = eye_c[:, None, :]
        gather[j, :, :, j, :] = eye_c[:, None, :]
        wide[j, j] = eye_c[:, :, None]
    out["spread"] = spread.reshape(4, 128, 128).astype(BF)
    out["gather"] = gather.reshape(4, C * C, 128).astype(BF)
    out["wide"] = wide.reshape(4, 128, C * C).astype(BF)
    return out


def dot(a, b):
    return jnp.dot(a, b, preferred_element_type=F32)


def dot_t(a, b):
    return lax.dot_general(a, b, (((1,), (1,)), ((), ())), preferred_element_type=F32)


def gelu_slope(v):
    cdf = 0.5 * (1.0 + lax.erf(v * 0.7071067811865476))
    return cdf + v * (0.3989422804014327 * jnp.exp(-0.5 * v * v))


def lane_group(rows):
    return lax.broadcasted_iota(jnp.int32, (rows, 128), 1) // C


def send_parts(parts, sent_ref):
    group = lane_group(8 * KS)
    for half in range(2):
        lanes = slice(half * 128, half * 128 + 128)
        turned = [parts[p, :, lanes] for p in range(4)]
        turned = [pltpu.roll(value, p * C, 1) if p else value for p, value in enumerate(turned)]
        for q in range(4):
            value = turned[(-q) % 4]
            for p in range(1, 4):
                value = jnp.where(group == p, turned[(p - q) % 4], value)
            if q:
                value = pltpu.roll(value, 128 - q * C, 1)
            for kz in range(KS):
                block, slot = divmod(2 * kz + half, 3)
                sent_ref[block, q, slot] = value[kz * 8 : kz * 8 + 8]


def analyse_grad_kernel(cot_ref, pre_ref, table_ref, zl_ref, sent_ref, even, odd, parts):
    step = pl.program_id(1)

    def cells(pair, flat):
        for x in range(4):
            for y in range(2):
                for j in range(4):
                    rows = slice(j * 16, j * 16 + 16)
                    v = pre_ref[0, x, 2 * pair + y, rows, :].astype(F32)
                    g = cot_ref[0, x, 2 * pair + y, rows, :].astype(F32)
                    at = (2 * x + y) * N + j * 16
                    flat[at : at + 16, :] = (g * gelu_slope(v)).astype(BF16)

    def analyse(pair, flat):
        sectioned = dot(zl_ref[...], flat[...]).astype(BF16)
        parts[pair] = dot(sectioned, table_ref[...])

    analyse((2 * step + 3) % 4, odd)
    cells(0, even)
    analyse(2 * step, even)
    cells(1, odd)

    @pl.when(step == 1)
    def _():
        analyse(3, odd)
        send_parts(parts, sent_ref)


def analyse_input_kernel(field_ref, table_ref, zl_ref, weight_ref, sent_ref, mix_ref, parts):
    step = pl.program_id(1)

    @pl.when((step == 0) & (pl.program_id(0) == 0))
    def _():
        rows = lax.broadcasted_iota(jnp.int32, (256, C), 0) % C
        copies = (rows == lax.broadcasted_iota(jnp.int32, (256, C), 1)).astype(BF16)
        mixed = dot_t(dot_t(copies, weight_ref[...]).astype(BF16), copies)
        blocks = [lax.broadcasted_iota(jnp.int32, (256, 256), axis) // C for axis in range(2)]
        mix_ref[...] = jnp.where(blocks[0] == blocks[1], mixed, 0.0).astype(BF16)
    for pair in range(2):
        field = field_ref[0, :, 2 * pair : 2 * pair + 2].reshape(8 * N, NT * C)
        sectioned = dot(zl_ref[...], field).astype(BF16)
        parts[2 * step + pair] = dot(sectioned, table_ref[...])

    @pl.when(step == 1)
    def _():
        send_parts(parts, sent_ref)


FIELD = pl.BlockSpec((1, 4, 4, N, NT * C), lambda b, p: (b, 0, p, 0, 0))
SENT = pl.BlockSpec((16, 4, 3, 8, 128), lambda b, p: (0, b, 0, 0, 0))
SENT_SHAPE = (16, 8, 3, 8, 128)
TILES = (6, 72, 128)
ANY = pl.BlockSpec(memory_space=pl.ANY)


def whole(shape):
    return pl.BlockSpec(shape, lambda *ids: (0,) * len(shape))


def params(limit):
    return pltpu.CompilerParams(vmem_limit_bytes=limit * MIB)


def cost(flops, nbytes):
    return pl.CostEstimate(flops=flops, bytes_accessed=nbytes, transcendentals=0)


def in_hbm(*arrays):
    return [pltpu.with_memory_space_constraint(a, pltpu.HBM) for a in arrays]


def analyse_grad(cotangent, pre_activation, k):
    return pl.pallas_call(
        analyse_grad_kernel,
        grid=(2, 2),
        in_specs=[FIELD, FIELD, whole((NT * C, MT * C)), whole((8 * KS, 8 * N))],
        out_specs=SENT,
        out_shape=pltpu.HBM(SENT_SHAPE, F32),
        scratch_shapes=[
            pltpu.VMEM((8 * N, NT * C), BF16),
            pltpu.VMEM((8 * N, NT * C), BF16),
            pltpu.VMEM((4, 8 * KS, MT * C), F32),
        ],
        compiler_params=params(24),
        cost_estimate=cost(4 * 10**9, 14 * 10**6),
        name="analyse_grad",
    )(*in_hbm(cotangent, pre_activation, k["table"], k["zl"]))


def mix_channels_kernel(cot_ref, pre_ref, mix_ref, out_ref, even, odd):
    def cells(pair, flat):
        for x in range(4):
            for y in range(2):
                for j in range(4):
                    rows = slice(j * 16, j * 16 + 16)
                    v = pre_ref[0, x, 2 * pair + y, rows, :].astype(F32)
                    g = cot_ref[0, x, 2 * pair + y, rows, :].astype(F32)
                    at = (2 * x + y) * N + j * 16
                    flat[at : at + 16, :] = (g * gelu_slope(v)).astype(BF16)

    def mix(pair, flat):
        for side in range(2):
            lanes = slice(side * 256, side * 256 + 256)
            mixed = dot(flat[:, lanes], mix_ref[...]).astype(BF16)
            out_ref[0, :, 2 * pair : 2 * pair + 2, :, lanes] = mixed.reshape(4, 2, N, 256)

    cells(0, even)
    mix(0, even)
    cells(1, odd)
    mix(1, odd)


def mix_channels(cotangent, pre_activation, mix):
    return pl.pallas_call(
        mix_channels_kernel,
        grid=(2, 2),
        in_specs=[FIELD, FIELD, whole((256, 256))],
        out_specs=FIELD,
        out_shape=pltpu.HBM(cotangent.shape, BF16),
        scratch_shapes=[pltpu.VMEM((8 * N, NT * C), BF16)] * 2,
        compiler_params=params(24),
        cost_estimate=cost(4 * 10**9, 12 * 10**6),
        name="mix_channels",
    )(*in_hbm(cotangent, pre_activation, mix))


def analyse_input(inputs, pointwise, k):
    return pl.pallas_call(
        analyse_input_kernel,
        grid=(2, 2),
        in_specs=[FIELD, whole((NT * C, MT * C)), whole((8 * KS, 8 * N)), whole((C, C))],
        out_specs=[SENT, whole((256, 256))],
        out_shape=[pltpu.HBM(SENT_SHAPE, F32), pltpu.HBM((256, 256), BF16)],
        scratch_shapes=[pltpu.VMEM((4, 8 * KS, MT * C), F32)],
        compiler_params=params(24),
        cost_estimate=cost(4 * 10**9, 6 * 10**6),
        name="analyse_input",
    )(*in_hbm(inputs, k["table"], k["zl"], pointwise))


def mode_of(j, t):
    return (j, t) if j < 3 else (t, 3)


def forward_kernel(got_ref, xl_ref, yb_hbm, keep_ref, cross_ref, yb_ref, fields, blocks, sem):
    me = lax.axis_index("gy")
    copy = pltpu.make_async_copy(yb_hbm.at[me], yb_ref, sem)
    copy.start()
    for slot in range(3):
        field = jnp.concatenate(
            [got_ref[:, d, slot].reshape(128, 128).astype(BF16) for d in range(8)], axis=1
        )
        wide = dot(xl_ref[...], jnp.concatenate([field, field], axis=0))
        for d in range(8):
            for half in range(2):
                rows = slice(d * 72 + slot * KS, d * 72 + slot * KS + KS)
                fields[rows, half * 128 : half * 128 + 128] = wide[
                    half * KS : half * KS + KS, d * 128 : d * 128 + 128
                ]
    copy.wait()
    group = lane_group(72)
    field = fields[...].astype(BF16)
    for to in range(8):
        part = dot(field, yb_ref[:, to * 128 : to * 128 + 128])
        for b in range(2):
            last = part[(4 * b + 3) * 72 : (4 * b + 4) * 72]
            for t in range(3):
                value = part[(4 * b + t) * 72 : (4 * b + t + 1) * 72]
                blocks[to, 3 * b + t] = jnp.where(group == 3, pltpu.roll(last, 96 - 32 * t, 1), value)
    for sx in range(4):
        keep_ref[sx] = blocks[me ^ (2 * sx)]
        cross_ref[sx] = blocks[me ^ (2 * sx + 1)]


def forward(got, k):
    vmem = pl.BlockSpec(memory_space=pltpu.VMEM)
    return pl.pallas_call(
        forward_kernel,
        in_specs=[vmem, vmem, ANY],
        out_shape=[jax.ShapeDtypeStruct((4, *TILES), F32)] * 2,
        scratch_shapes=[
            pltpu.VMEM((256, 1024), BF16),
            pltpu.VMEM((576, 256), F32),
            pltpu.VMEM((8, *TILES), F32),
            pltpu.SemaphoreType.DMA,
        ],
        compiler_params=params(16),
        cost_estimate=cost(10**9, 4 * 10**6),
        name="forward",
    )(got, k["xl"], *in_hbm(k["yb"]))


def add_cores_kernel(keep_ref, cross_ref, *outs):
    for sx in range(4):
        outs[sx][...] = keep_ref[sx] + cross_ref[sx]


def add_cores(keep, cross):
    return pl.pallas_call(
        add_cores_kernel,
        out_shape=[jax.ShapeDtypeStruct(TILES, F32)] * 4,
        compiler_params=params(16),
        cost_estimate=cost(10**6, 10**6),
        name="add_cores",
    )(keep, cross)


def across(block, sx):
    return lax.ppermute(block, "gy", [(i, i ^ sx) for i in range(8)])


def reduce_cores(blocks):
    keep, cross = blocks
    return add_cores(keep, across(cross, 1))


def reduce_chips(sums):
    own, *others = sums
    return [own] + [across(other, 2 * sx + 2) for sx, other in enumerate(others)]


def gather_second(block):
    parts = [block, across(block, 1)]
    for sx in range(1, 4):
        far = across(block, 2 * sx)
        parts += [far, across(far, 1)]
    return parts


def transform_x(got_ref, xl_ref, planes):
    for slot in range(3):
        field = jnp.concatenate(
            [got_ref[:, s, slot].reshape(128, 128).astype(BF16) for s in range(8)], axis=1
        )
        wide = dot(xl_ref[...], jnp.concatenate([field, field], axis=0))
        for s in range(8):
            planes[s, slot * 48 : slot * 48 + 48, :] = wide[:, s * 128 : s * 128 + 128]


def transform_y(planes, cy_ref, blocks):
    group = lane_group(72)

    def block(d, carry):
        totals = [jnp.zeros((72, 128), F32)] * 3
        for s in range(8):
            for half in range(2):
                starts = [slot * 48 + half * KS for slot in range(3)]
                rows = jnp.concatenate([planes[s, at : at + KS, :] for at in starts], axis=0)
                for j in range(3):
                    totals[j] = totals[j] + rows * cy_ref[d, j, half * 8 + s : half * 8 + s + 1, :]
        value = jnp.zeros((72, 128), F32)
        for j in range(3):
            total = totals[j] + pltpu.roll(totals[j], 64, 1)
            total = total + pltpu.roll(total, 32, 1)
            value = jnp.where(group == j, total, value)
        blocks[d] = value
        return carry

    lax.fori_loop(0, 8, block, 0)


def group_shape(rows):
    return jax.ShapeDtypeStruct((4, rows, 128), F32)


def deal(blocks, keep_ref, cross_ref):
    me = lax.axis_index("gy")
    for sx in range(4):
        keep_ref[sx] = blocks[me ^ (2 * sx)]
        cross_ref[sx] = blocks[me ^ (2 * sx + 1)]


def arrived(refs):
    keep, cross, *far = refs
    return [keep.at[0], cross.at[0]] + [ref.at[i] for ref in far for i in range(2)]


def collect(parts, blocks):
    me = lax.axis_index("gy")
    for s in range(8):
        blocks[me ^ s] = parts[s][...]


def planes_kernel(got_ref, xl_ref, cy_hbm, keep_ref, cross_ref, cy_ref, planes, blocks, sem):
    copy = pltpu.make_async_copy(cy_hbm, cy_ref, sem)
    copy.start()
    transform_x(got_ref, xl_ref, planes)
    copy.wait()
    transform_y(planes, cy_ref, blocks)
    deal(blocks, keep_ref, cross_ref)


def planes(got, k):
    vmem = pl.BlockSpec(memory_space=pltpu.VMEM)
    return pl.pallas_call(
        planes_kernel,
        in_specs=[vmem, vmem, ANY],
        out_shape=[group_shape(72)] * 2,
        scratch_shapes=[
            pltpu.VMEM((8, 3, 16, 128), F32),
            pltpu.VMEM((8, 144, 128), F32),
            pltpu.VMEM((8, 72, 128), F32),
            pltpu.SemaphoreType.DMA,
        ],
        compiler_params=params(16),
        cost_estimate=cost(10**9, 3 * 10**6),
        name="planes",
    )(got, k["xl"], *in_hbm(k["cy"]))


def pair_up_kernel(keep_ref, cross_ref, *outs):
    for sx in range(1, 4):
        outs[sx - 1][0] = keep_ref[sx]
        outs[sx - 1][1] = cross_ref[sx]


def pair_up(keep, cross):
    shape = jax.ShapeDtypeStruct((2, *keep.shape[1:]), F32)
    return pl.pallas_call(
        pair_up_kernel,
        out_shape=[shape] * 3,
        compiler_params=params(16),
        cost_estimate=cost(10**6, 10**6),
        name="pair_up",
    )(keep, cross)


def exchange_second(blocks):
    keep, cross = blocks
    cross = across(cross, 1)
    pairs = pair_up(keep, cross)
    return [keep, cross] + [across(pair, 2 * sx + 2) for sx, pair in enumerate(pairs)]


def mode_grad_kernel(*refs):
    parts, (spread_ref, weight_hbm, gather_hbm, yb_hbm) = arrived(refs[:5]), refs[5:9]
    out_ref, grads_ref, yb_ref, weight_ref, gather_ref, sems = refs[9:]
    copies = []
    for ky in range(3):
        copies.append(pltpu.make_async_copy(weight_hbm.at[ky], weight_ref.at[ky], sems.at[0, ky]))
        copies.append(pltpu.make_async_copy(gather_hbm.at[ky], gather_ref.at[ky], sems.at[1, ky]))
    copies.append(pltpu.make_async_copy(yb_hbm.at[lax.axis_index("gy")], yb_ref, sems.at[0, 3]))
    for copy in copies:
        copy.start()
    collect(parts, grads_ref)
    field = []
    for b in range(2):
        for slot in range(3):
            for q in range(4):
                field.append(grads_ref[4 * b + q, slot * KS : slot * KS + KS, :])
    field = jnp.concatenate(field, axis=0).astype(BF16)
    total = None
    for ky in range(3):
        lanes = dot(field, spread_ref[ky]).astype(BF16)
        copies[2 * ky].wait()
        products = []
        for b in range(2):
            copy = lanes[b * 288 : b * 288 + 288]
            products.append(weight_ref[ky] * jnp.concatenate([copy] * 8, axis=1))
        copies[2 * ky + 1].wait()
        term = dot(jnp.concatenate(products, axis=0), gather_ref[ky])
        total = term if total is None else total + term
    group = lane_group(72)
    for b in range(2):
        modes = []
        for q in range(4):
            starts = [b * 288 + (slot * 4 + q) * KS for slot in range(3)]
            modes.append(jnp.concatenate([total[at : at + KS] for at in starts], axis=0))
        for t in range(3):
            out_ref[3 * b + t] = jnp.where(group == 3, pltpu.roll(modes[3], 96 - 32 * t, 1), modes[t])
    copies[6].wait()


def mode_grad(parts, weights, k):
    vmem = pl.BlockSpec(memory_space=pltpu.VMEM)
    return pl.pallas_call(
        mode_grad_kernel,
        in_specs=[vmem] * 6 + [ANY] * 3,
        out_shape=[
            jax.ShapeDtypeStruct(TILES, F32),
            jax.ShapeDtypeStruct((8, 72, 128), F32),
            pltpu.VMEM((1024, 256), BF16),
        ],
        scratch_shapes=[
            pltpu.VMEM((3, 12 * KS, C * C), BF16),
            pltpu.VMEM((4, C * C, 128), BF16),
            pltpu.SemaphoreType.DMA((2, 4)),
        ],
        compiler_params=params(16),
        cost_estimate=cost(10**9, 4 * 10**6),
        name="mode_grad",
    )(*parts, k["spread"], *in_hbm(weights.reshape(3, 12 * KS, C * C), k["gather"], k["yb_t"]))


def backward_kernel(*refs):
    parts, (xl_ref, yb_ref, sent_hbm, blocks, sent, sems) = refs[:8], refs[8:]
    me = lax.axis_index("gy")
    for s in range(8):
        blocks[me ^ s] = parts[s][...]
    group = lane_group(72)
    columns = []
    for s in range(8):
        tiles = []
        for b in range(2):
            three = [blocks[s, 3 * b + t] for t in range(3)]
            last = pltpu.roll(three[0], 32, 1)
            for t in range(1, 3):
                last = jnp.where(group == t, pltpu.roll(three[t], 32 + 32 * t, 1), last)
            tiles += three + [last]
        columns.append(jnp.concatenate(tiles, axis=0).astype(BF16))
    wide = dot(jnp.concatenate(columns, axis=1), yb_ref[...]).astype(BF16)
    copies = []
    for slot in range(3):
        both = []
        for d in range(8):
            rows = wide[d * 72 + slot * KS : d * 72 + slot * KS + KS]
            both.append(jnp.concatenate([rows[:, :128], rows[:, 128:]], axis=0))
        both = jnp.concatenate(both, axis=1)
        out = dot(xl_ref[...], jnp.concatenate([both, both], axis=0))
        for d in range(8):
            sent[slot, :, d] = out[:, d * 128 : d * 128 + 128].reshape(16, 8, 128)
        copies.append(pltpu.make_async_copy(sent.at[slot], sent_hbm.at[:, :, slot], sems.at[slot]))
        copies[-1].start()
    for copy in copies:
        copy.wait()


def backward(parts, yb, k):
    return pl.pallas_call(
        backward_kernel,
        out_shape=pltpu.HBM(SENT_SHAPE, F32),
        out_specs=ANY,
        scratch_shapes=[
            pltpu.VMEM((8, *TILES), F32),
            pltpu.VMEM((3, 16, 8, 8, 128), F32),
            pltpu.SemaphoreType.DMA((3,)),
        ],
        compiler_params=params(16),
        cost_estimate=cost(10**9, 4 * 10**6),
        name="backward",
    )(*parts, k["xl_t"], yb)


def spectral_grad_kernel(grads_ref, *refs):
    fields, (spread_ref, wide_ref, out_ref) = refs[:4], refs[4:]
    ky = pl.program_id(0)

    def tile(t):
        value = fields[0][t] + fields[1][t] + fields[2][t] + fields[3][t]
        return value.astype(BF16)

    copies = dot(grads_ref[...].reshape(576, 128).astype(BF16), spread_ref[ky])
    for q in range(4):
        j, t = (ky, q) if q < 3 else (3, ky)
        field = jnp.concatenate([tile(t), tile(3 + t)], axis=0)
        wide = dot(field, wide_ref[j])
        for slot in range(3):
            total = None
            for b in range(2):
                at = b * 72 + slot * KS
                source = (4 * b + q) * 72 + slot * KS
                copy = copies[source : source + KS]
                term = wide[at : at + KS] * jnp.concatenate([copy] * 8, axis=1)
                total = term if total is None else total + term
            out_ref[0, slot * 4 + q] = total


def spectral_grad(grads, fields, k):
    return pl.pallas_call(
        spectral_grad_kernel,
        grid=(3,),
        in_specs=[whole((8, 72, 128))]
        + [whole(TILES)] * 4
        + [whole((4, 128, 128)), whole((4, 128, C * C))],
        out_specs=pl.BlockSpec((1, 12, KS, C * C), lambda i: (i, 0, 0, 0)),
        out_shape=pltpu.HBM((3, 12, KS, C * C), F32),
        compiler_params=params(24),
        cost_estimate=cost(10**9, 4 * 10**6),
        name="spectral_grad",
    )(grads, *fields, *in_hbm(k["spread"], k["wide"]))


def synthesise_kernel(got_ref, table_ref, zl_ref, mixed_hbm, out_hbm, mixed, out, parts, in_sems, out_sems):
    def incoming(n):
        return pltpu.make_async_copy(mixed_hbm.at[n // 4, :, pl.ds(2 * (n % 4), 2)], mixed.at[n], in_sems.at[n])

    def outgoing(n):
        return pltpu.make_async_copy(out.at[n], out_hbm.at[n // 4, :, pl.ds(2 * (n % 4), 2)], out_sems.at[n])

    for n in range(8):
        incoming(n).start()

    def gather(b):
        group = lane_group(8 * KS)
        for half in range(2):
            turned = []
            for q in range(4):
                tiles = []
                for kz in range(KS):
                    block, slot = divmod(2 * kz + half, 3)
                    tiles.append(got_ref[block, 4 * b + q, slot])
                value = jnp.concatenate(tiles, axis=0)
                turned.append(pltpu.roll(value, q * C, 1) if q else value)
            for p in range(4):
                value = turned[(-p) % 4]
                for g in range(1, 4):
                    value = jnp.where(group == g, turned[(g - p) % 4], value)
                value = pltpu.roll(value, 128 - p * C, 1) if p else value
                parts[p, :, half * 128 : half * 128 + 128] = value.astype(BF16)

    def chunk(n, carry):
        @pl.when(n % 4 == 0)
        def _():
            gather(n // 4)

        incoming(n).wait()
        timed = dot(parts[n % 4], table_ref[...]).astype(BF16)
        value = dot(zl_ref[...], timed).reshape(4, 2, N, NT * C)
        out[n] = (value + mixed[n].astype(F32)).astype(BF16)
        outgoing(n).start()
        return carry

    lax.fori_loop(0, 8, chunk, 0)
    for n in range(8):
        outgoing(n).wait()


def synthesise(got, mixed, k):
    vmem = pl.BlockSpec(memory_space=pltpu.VMEM)
    return pl.pallas_call(
        synthesise_kernel,
        in_specs=[vmem, vmem, vmem, ANY],
        out_specs=ANY,
        out_shape=pltpu.HBM(mixed.shape, BF16),
        scratch_shapes=[
            pltpu.VMEM((8, 4, 2, N, NT * C), BF16),
            pltpu.VMEM((8, 4, 2, N, NT * C), BF16),
            pltpu.VMEM((4, 8 * KS, MT * C), BF16),
            pltpu.SemaphoreType.DMA((8,)),
            pltpu.SemaphoreType.DMA((8,)),
        ],
        compiler_params=params(24),
        cost_estimate=cost(4 * 10**9, 10 * 10**6),
        name="synthesise",
    )(got, k["table_t"], k["zl_t"], *in_hbm(mixed))


def exchange_all(block):
    flat = block.reshape(128, 24, 128)
    return lax.all_to_all(flat, ("gx", "gy"), 0, 0, tiled=True).reshape(block.shape)


def exchange_first(block):
    flat = block.reshape(16, 192, 128)
    return lax.all_to_all(flat, "gx", 0, 0, tiled=True).reshape(block.shape)


def body(inputs, cotangent, pre_activation, pointwise, spectral):
    k = constants()
    weights = jnp.transpose(spectral, (1, 2, 0, 3))
    sent = analyse_grad(cotangent, pre_activation, k)
    got = exchange_all(sent)
    sent_input, mix = analyse_input(inputs, pointwise, k)
    mixed = mix_channels(cotangent, pre_activation, mix)
    got, *_ = lax.optimization_barrier((got, sent_input, mixed))
    blocks = planes(got, k)
    sent_input, *_ = lax.optimization_barrier((sent_input, blocks[0]))
    got_input = exchange_first(sent_input)
    modes, grads, yb = mode_grad(exchange_second(blocks), weights, k)
    got_input, *_ = lax.optimization_barrier((got_input, modes))
    sums = reduce_cores(forward(got_input, k))
    back = exchange_first(backward(gather_second(modes), yb, k))
    weight_grad = spectral_grad(grads, reduce_chips(sums), k)
    back, *_ = lax.optimization_barrier((back, weight_grad))
    return synthesise(back, mixed, k), jnp.transpose(weight_grad, (2, 0, 1, 3))


def solution(mesh):
    in_specs = (
        P(None, "gx", "gy", None, None),
        P(None, "gx", "gy", None, None),
        P(None, "gx", "gy", None, None),
        P(),
        P(None, "gy", "gx", None),
    )
    out_specs = (P(None, "gx", "gy", None, None), P(None, "gy", "gx", None))
    return jax.shard_map(body, mesh=mesh, in_specs=in_specs, out_specs=out_specs, check_vma=False)
```

```python
import functools
import math

import jax
import jax.numpy as jnp
import ml_dtypes
import numpy as np
from jax import lax
from jax.experimental import pallas as pl
from jax.experimental.pallas import tpu as pltpu
from jax.sharding import PartitionSpec as P

N = 64
NT = 16
MS = 12
MT = 8
KS = 24
C = 32
BF = ml_dtypes.bfloat16
F32 = jnp.float32
BF16 = jnp.bfloat16
MIB = 1 << 20


def fourier(length, frequencies):
    points = np.arange(length, dtype=np.float64)[:, None]
    orders = np.arange(frequencies, dtype=np.float64)[None, :]
    scales = np.where(orders == 0.0, math.sqrt(1.0 / length), math.sqrt(2.0 / length))
    cosines = scales * np.cos(2.0 * math.pi * points * orders / length)
    sines = math.sqrt(2.0 / length) * np.sin(2.0 * math.pi * points * (orders + 1.0) / length)
    return np.concatenate([cosines, sines], axis=1).astype(np.float32)


def cosine(length, modes):
    points = np.arange(length, dtype=np.float64)[:, None]
    orders = np.arange(modes, dtype=np.float64)[None, :]
    scales = np.where(orders == 0.0, math.sqrt(1.0 / length), math.sqrt(2.0 / length))
    return (scales * np.cos(math.pi * orders * (points + 0.5) / length)).astype(np.float32)


def constants():
    basis = fourier(N, MS)
    third = basis.astype(BF).astype(np.float32)
    time = cosine(NT, MT).astype(BF).astype(np.float32)
    eye_c = np.eye(C, dtype=np.float32)
    eye_r = np.eye(8, dtype=np.float32)
    out = {}
    table = np.einsum("tm,cd->tcmd", time, eye_c).reshape(NT * C, MT * C)
    out["table"] = table.astype(BF)
    out["table_t"] = table.T.copy().astype(BF)
    zl = np.einsum("zk,rs->krsz", third, eye_r).reshape(KS * 8, 8 * N)
    out["zl"] = zl.astype(BF)
    out["zl_t"] = zl.T.copy().astype(BF)
    high = basis.astype(BF).astype(np.float32)
    low = (basis - high).astype(BF).astype(np.float32)
    eye_h = np.eye(2, dtype=np.float32)
    forms = [np.einsum("xk,hg->hkxg", part, eye_h).reshape(2 * KS, 2 * N) for part in (high, low)]
    out["xl"] = np.concatenate(forms, axis=1).astype(BF)
    out["xl_t"] = np.concatenate([form.T for form in forms], axis=1).astype(BF)
    padded = np.zeros((N, 8, 4), np.float32)
    padded[:, :, :3] = basis.reshape(N, 8, 3)
    yb = np.einsum("slhdk,ce->shlcdke", padded.reshape(8, 4, 2, 8, 4), eye_c)
    yb = yb.reshape(8, 256, 1024).astype(BF)
    out["yb"] = yb
    out["yb_t"] = np.swapaxes(yb, 1, 2).copy()
    second = basis.reshape(8, 4, 2, 8, 3)
    out["cy"] = np.repeat(np.einsum("slhdj->djhsl", second).reshape(8, 3, 16, 4), C, axis=3)
    spread = np.zeros((4, 4, C, 4, C), np.float32)
    gather = np.zeros((4, C, C, 4, C), np.float32)
    wide = np.zeros((4, 4, C, C, C), np.float32)
    for j in range(4):
        spread[j, j] = eye_c[:, None, :]
        gather[j, :, :, j, :] = eye_c[:, None, :]
        wide[j, j] = eye_c[:, :, None]
    out["spread"] = spread.reshape(4, 128, 128).astype(BF)
    out["gather"] = gather.reshape(4, C * C, 128).astype(BF)
    out["wide"] = wide.reshape(4, 128, C * C).astype(BF)
    return out


def dot(a, b):
    return jnp.dot(a, b, preferred_element_type=F32)


def dot_t(a, b):
    return lax.dot_general(a, b, (((1,), (1,)), ((), ())), preferred_element_type=F32)


def gelu_slope(v):
    cdf = 0.5 * (1.0 + lax.erf(v * 0.7071067811865476))
    return cdf + v * (0.3989422804014327 * jnp.exp(-0.5 * v * v))


def lane_group(rows):
    return lax.broadcasted_iota(jnp.int32, (rows, 128), 1) // C


def send_parts(parts, sent_ref):
    group = lane_group(8 * KS)
    for half in range(2):
        lanes = slice(half * 128, half * 128 + 128)
        turned = [parts[p, :, lanes] for p in range(4)]
        turned = [pltpu.roll(value, p * C, 1) if p else value for p, value in enumerate(turned)]
        for q in range(4):
            value = turned[(-q) % 4]
            for p in range(1, 4):
                value = jnp.where(group == p, turned[(p - q) % 4], value)
            if q:
                value = pltpu.roll(value, 128 - q * C, 1)
            for kz in range(KS):
                block, slot = divmod(2 * kz + half, 3)
                sent_ref[block, q, slot] = value[kz * 8 : kz * 8 + 8]


def analyse_grad_kernel(cot_ref, pre_ref, table_ref, zl_ref, sent_ref, even, odd, parts):
    step = pl.program_id(1)

    def cells(pair, flat):
        for x in range(4):
            for y in range(2):
                for j in range(4):
                    rows = slice(j * 16, j * 16 + 16)
                    v = pre_ref[0, x, 2 * pair + y, rows, :].astype(F32)
                    g = cot_ref[0, x, 2 * pair + y, rows, :].astype(F32)
                    at = (2 * x + y) * N + j * 16
                    flat[at : at + 16, :] = (g * gelu_slope(v)).astype(BF16)

    def analyse(pair, flat):
        sectioned = dot(zl_ref[...], flat[...]).astype(BF16)
        parts[pair] = dot(sectioned, table_ref[...])

    analyse((2 * step + 3) % 4, odd)
    cells(0, even)
    analyse(2 * step, even)
    cells(1, odd)

    @pl.when(step == 1)
    def _():
        analyse(3, odd)
        send_parts(parts, sent_ref)


def analyse_input_kernel(field_ref, table_ref, zl_ref, weight_ref, sent_ref, mix_ref, parts):
    step = pl.program_id(1)

    @pl.when((step == 0) & (pl.program_id(0) == 0))
    def _():
        rows = lax.broadcasted_iota(jnp.int32, (256, C), 0) % C
        copies = (rows == lax.broadcasted_iota(jnp.int32, (256, C), 1)).astype(BF16)
        mixed = dot_t(dot_t(copies, weight_ref[...]).astype(BF16), copies)
        blocks = [lax.broadcasted_iota(jnp.int32, (256, 256), axis) // C for axis in range(2)]
        mix_ref[...] = jnp.where(blocks[0] == blocks[1], mixed, 0.0).astype(BF16)
    for pair in range(2):
        field = field_ref[0, :, 2 * pair : 2 * pair + 2].reshape(8 * N, NT * C)
        sectioned = dot(zl_ref[...], field).astype(BF16)
        parts[2 * step + pair] = dot(sectioned, table_ref[...])

    @pl.when(step == 1)
    def _():
        send_parts(parts, sent_ref)


FIELD = pl.BlockSpec((1, 4, 4, N, NT * C), lambda b, p: (b, 0, p, 0, 0))
SENT = pl.BlockSpec((16, 4, 3, 8, 128), lambda b, p: (0, b, 0, 0, 0))
SENT_SHAPE = (16, 8, 3, 8, 128)
TILES = (6, 72, 128)
ANY = pl.BlockSpec(memory_space=pl.ANY)


def whole(shape):
    return pl.BlockSpec(shape, lambda *ids: (0,) * len(shape))


def params(limit):
    return pltpu.CompilerParams(vmem_limit_bytes=limit * MIB)


def cost(flops, nbytes):
    return pl.CostEstimate(flops=flops, bytes_accessed=nbytes, transcendentals=0)


def in_hbm(*arrays):
    return [pltpu.with_memory_space_constraint(a, pltpu.HBM) for a in arrays]


def analyse_grad(cotangent, pre_activation, k):
    return pl.pallas_call(
        analyse_grad_kernel,
        grid=(2, 2),
        in_specs=[FIELD, FIELD, whole((NT * C, MT * C)), whole((8 * KS, 8 * N))],
        out_specs=SENT,
        out_shape=pltpu.HBM(SENT_SHAPE, F32),
        scratch_shapes=[
            pltpu.VMEM((8 * N, NT * C), BF16),
            pltpu.VMEM((8 * N, NT * C), BF16),
            pltpu.VMEM((4, 8 * KS, MT * C), F32),
        ],
        compiler_params=params(24),
        cost_estimate=cost(4 * 10**9, 14 * 10**6),
        name="analyse_grad",
    )(*in_hbm(cotangent, pre_activation, k["table"], k["zl"]))


def mix_channels_kernel(cot_ref, pre_ref, mix_ref, out_ref, even, odd):
    def cells(pair, flat):
        for x in range(4):
            for y in range(2):
                for j in range(4):
                    rows = slice(j * 16, j * 16 + 16)
                    v = pre_ref[0, x, 2 * pair + y, rows, :].astype(F32)
                    g = cot_ref[0, x, 2 * pair + y, rows, :].astype(F32)
                    at = (2 * x + y) * N + j * 16
                    flat[at : at + 16, :] = (g * gelu_slope(v)).astype(BF16)

    def mix(pair, flat):
        for side in range(2):
            lanes = slice(side * 256, side * 256 + 256)
            mixed = dot(flat[:, lanes], mix_ref[...]).astype(BF16)
            out_ref[0, :, 2 * pair : 2 * pair + 2, :, lanes] = mixed.reshape(4, 2, N, 256)

    cells(0, even)
    mix(0, even)
    cells(1, odd)
    mix(1, odd)


def mix_channels(cotangent, pre_activation, mix):
    return pl.pallas_call(
        mix_channels_kernel,
        grid=(2, 2),
        in_specs=[FIELD, FIELD, whole((256, 256))],
        out_specs=FIELD,
        out_shape=pltpu.HBM(cotangent.shape, BF16),
        scratch_shapes=[pltpu.VMEM((8 * N, NT * C), BF16)] * 2,
        compiler_params=params(24),
        cost_estimate=cost(4 * 10**9, 12 * 10**6),
        name="mix_channels",
    )(*in_hbm(cotangent, pre_activation, mix))


def analyse_input(inputs, pointwise, k):
    return pl.pallas_call(
        analyse_input_kernel,
        grid=(2, 2),
        in_specs=[FIELD, whole((NT * C, MT * C)), whole((8 * KS, 8 * N)), whole((C, C))],
        out_specs=[SENT, whole((256, 256))],
        out_shape=[pltpu.HBM(SENT_SHAPE, F32), pltpu.HBM((256, 256), BF16)],
        scratch_shapes=[pltpu.VMEM((4, 8 * KS, MT * C), F32)],
        compiler_params=params(24),
        cost_estimate=cost(4 * 10**9, 6 * 10**6),
        name="analyse_input",
    )(*in_hbm(inputs, k["table"], k["zl"], pointwise))


def mode_of(j, t):
    return (j, t) if j < 3 else (t, 3)


def forward_kernel(got_ref, xl_ref, yb_hbm, keep_ref, cross_ref, yb_ref, fields, blocks, sem):
    me = lax.axis_index("gy")
    copy = pltpu.make_async_copy(yb_hbm.at[me], yb_ref, sem)
    copy.start()
    for slot in range(3):
        field = jnp.concatenate(
            [got_ref[:, d, slot].reshape(128, 128).astype(BF16) for d in range(8)], axis=1
        )
        wide = dot(xl_ref[...], jnp.concatenate([field, field], axis=0))
        for d in range(8):
            for half in range(2):
                rows = slice(d * 72 + slot * KS, d * 72 + slot * KS + KS)
                fields[rows, half * 128 : half * 128 + 128] = wide[
                    half * KS : half * KS + KS, d * 128 : d * 128 + 128
                ]
    copy.wait()
    group = lane_group(72)
    field = fields[...].astype(BF16)
    for to in range(8):
        part = dot(field, yb_ref[:, to * 128 : to * 128 + 128])
        for b in range(2):
            last = part[(4 * b + 3) * 72 : (4 * b + 4) * 72]
            for t in range(3):
                value = part[(4 * b + t) * 72 : (4 * b + t + 1) * 72]
                blocks[to, 3 * b + t] = jnp.where(group == 3, pltpu.roll(last, 96 - 32 * t, 1), value)
    for sx in range(4):
        keep_ref[sx] = blocks[me ^ (2 * sx)]
        cross_ref[sx] = blocks[me ^ (2 * sx + 1)]


def forward(got, k):
    vmem = pl.BlockSpec(memory_space=pltpu.VMEM)
    return pl.pallas_call(
        forward_kernel,
        in_specs=[vmem, vmem, ANY],
        out_shape=[jax.ShapeDtypeStruct((4, *TILES), F32)] * 2,
        scratch_shapes=[
            pltpu.VMEM((256, 1024), BF16),
            pltpu.VMEM((576, 256), F32),
            pltpu.VMEM((8, *TILES), F32),
            pltpu.SemaphoreType.DMA,
        ],
        compiler_params=params(16),
        cost_estimate=cost(10**9, 4 * 10**6),
        name="forward",
    )(got, k["xl"], *in_hbm(k["yb"]))


def add_cores_kernel(keep_ref, cross_ref, *outs):
    for sx in range(4):
        outs[sx][...] = keep_ref[sx] + cross_ref[sx]


def add_cores(keep, cross):
    return pl.pallas_call(
        add_cores_kernel,
        out_shape=[jax.ShapeDtypeStruct(TILES, F32)] * 4,
        compiler_params=params(16),
        cost_estimate=cost(10**6, 10**6),
        name="add_cores",
    )(keep, cross)


def across(block, sx):
    return lax.ppermute(block, "gy", [(i, i ^ sx) for i in range(8)])


def reduce_cores(blocks):
    keep, cross = blocks
    return add_cores(keep, across(cross, 1))


def reduce_chips(sums):
    own, *others = sums
    return [own] + [across(other, 2 * sx + 2) for sx, other in enumerate(others)]


def gather_second(block):
    parts = [block, across(block, 1)]
    for sx in range(1, 4):
        far = across(block, 2 * sx)
        parts += [far, across(far, 1)]
    return parts


def transform_x(got_ref, xl_ref, planes):
    for slot in range(3):
        field = jnp.concatenate(
            [got_ref[:, s, slot].reshape(128, 128).astype(BF16) for s in range(8)], axis=1
        )
        wide = dot(xl_ref[...], jnp.concatenate([field, field], axis=0))
        for s in range(8):
            planes[s, slot * 48 : slot * 48 + 48, :] = wide[:, s * 128 : s * 128 + 128]


def transform_y(planes, cy_ref, blocks):
    group = lane_group(72)

    def block(d, carry):
        totals = [jnp.zeros((72, 128), F32)] * 3
        for s in range(8):
            for half in range(2):
                starts = [slot * 48 + half * KS for slot in range(3)]
                rows = jnp.concatenate([planes[s, at : at + KS, :] for at in starts], axis=0)
                for j in range(3):
                    totals[j] = totals[j] + rows * cy_ref[d, j, half * 8 + s : half * 8 + s + 1, :]
        value = jnp.zeros((72, 128), F32)
        for j in range(3):
            total = totals[j] + pltpu.roll(totals[j], 64, 1)
            total = total + pltpu.roll(total, 32, 1)
            value = jnp.where(group == j, total, value)
        blocks[d] = value
        return carry

    lax.fori_loop(0, 8, block, 0)


def group_shape(rows):
    return jax.ShapeDtypeStruct((4, rows, 128), F32)


def deal(blocks, keep_ref, cross_ref):
    me = lax.axis_index("gy")
    for sx in range(4):
        keep_ref[sx] = blocks[me ^ (2 * sx)]
        cross_ref[sx] = blocks[me ^ (2 * sx + 1)]


def arrived(refs):
    keep, cross, *far = refs
    return [keep.at[0], cross.at[0]] + [ref.at[i] for ref in far for i in range(2)]


def collect(parts, blocks):
    me = lax.axis_index("gy")
    for s in range(8):
        blocks[me ^ s] = parts[s][...]


def planes_kernel(got_ref, xl_ref, cy_hbm, keep_ref, cross_ref, cy_ref, planes, blocks, sem):
    copy = pltpu.make_async_copy(cy_hbm, cy_ref, sem)
    copy.start()
    transform_x(got_ref, xl_ref, planes)
    copy.wait()
    transform_y(planes, cy_ref, blocks)
    deal(blocks, keep_ref, cross_ref)


def planes(got, k):
    vmem = pl.BlockSpec(memory_space=pltpu.VMEM)
    return pl.pallas_call(
        planes_kernel,
        in_specs=[vmem, vmem, ANY],
        out_shape=[group_shape(72)] * 2,
        scratch_shapes=[
            pltpu.VMEM((8, 3, 16, 128), F32),
            pltpu.VMEM((8, 144, 128), F32),
            pltpu.VMEM((8, 72, 128), F32),
            pltpu.SemaphoreType.DMA,
        ],
        compiler_params=params(16),
        cost_estimate=cost(10**9, 3 * 10**6),
        name="planes",
    )(got, k["xl"], *in_hbm(k["cy"]))


def pair_up_kernel(keep_ref, cross_ref, *outs):
    for sx in range(1, 4):
        outs[sx - 1][0] = keep_ref[sx]
        outs[sx - 1][1] = cross_ref[sx]


def pair_up(keep, cross):
    shape = jax.ShapeDtypeStruct((2, *keep.shape[1:]), F32)
    return pl.pallas_call(
        pair_up_kernel,
        out_shape=[shape] * 3,
        compiler_params=params(16),
        cost_estimate=cost(10**6, 10**6),
        name="pair_up",
    )(keep, cross)


def exchange_second(blocks):
    keep, cross = blocks
    cross = across(cross, 1)
    pairs = pair_up(keep, cross)
    return [keep, cross] + [across(pair, 2 * sx + 2) for sx, pair in enumerate(pairs)]


def mode_grad_kernel(*refs):
    parts, (spread_ref, weight_hbm, gather_hbm, yb_hbm) = arrived(refs[:5]), refs[5:9]
    out_ref, grads_ref, yb_ref, weight_ref, gather_ref, sems = refs[9:]
    copies = []
    for ky in range(3):
        copies.append(pltpu.make_async_copy(weight_hbm.at[ky], weight_ref.at[ky], sems.at[0, ky]))
        copies.append(pltpu.make_async_copy(gather_hbm.at[ky], gather_ref.at[ky], sems.at[1, ky]))
    copies.append(pltpu.make_async_copy(yb_hbm.at[lax.axis_index("gy")], yb_ref, sems.at[0, 3]))
    for copy in copies:
        copy.start()
    collect(parts, grads_ref)
    field = []
    for b in range(2):
        for slot in range(3):
            for q in range(4):
                field.append(grads_ref[4 * b + q, slot * KS : slot * KS + KS, :])
    field = jnp.concatenate(field, axis=0).astype(BF16)
    total = None
    for ky in range(3):
        lanes = dot(field, spread_ref[ky]).astype(BF16)
        copies[2 * ky].wait()
        products = []
        for b in range(2):
            copy = lanes[b * 288 : b * 288 + 288]
            products.append(weight_ref[ky] * jnp.concatenate([copy] * 8, axis=1))
        copies[2 * ky + 1].wait()
        term = dot(jnp.concatenate(products, axis=0), gather_ref[ky])
        total = term if total is None else total + term
    group = lane_group(72)
    for b in range(2):
        modes = []
        for q in range(4):
            starts = [b * 288 + (slot * 4 + q) * KS for slot in range(3)]
            modes.append(jnp.concatenate([total[at : at + KS] for at in starts], axis=0))
        for t in range(3):
            out_ref[3 * b + t] = jnp.where(group == 3, pltpu.roll(modes[3], 96 - 32 * t, 1), modes[t])
    copies[6].wait()


def mode_grad(parts, weights, k):
    vmem = pl.BlockSpec(memory_space=pltpu.VMEM)
    return pl.pallas_call(
        mode_grad_kernel,
        in_specs=[vmem] * 6 + [ANY] * 3,
        out_shape=[
            jax.ShapeDtypeStruct(TILES, F32),
            jax.ShapeDtypeStruct((8, 72, 128), F32),
            pltpu.VMEM((1024, 256), BF16),
        ],
        scratch_shapes=[
            pltpu.VMEM((3, 12 * KS, C * C), BF16),
            pltpu.VMEM((4, C * C, 128), BF16),
            pltpu.SemaphoreType.DMA((2, 4)),
        ],
        compiler_params=params(16),
        cost_estimate=cost(10**9, 4 * 10**6),
        name="mode_grad",
    )(*parts, k["spread"], *in_hbm(weights.reshape(3, 12 * KS, C * C), k["gather"], k["yb_t"]))


def backward_kernel(*refs):
    parts, (xl_ref, yb_ref, sent_hbm, blocks, sent, sems) = refs[:8], refs[8:]
    me = lax.axis_index("gy")
    for s in range(8):
        blocks[me ^ s] = parts[s][...]
    group = lane_group(72)
    columns = []
    for s in range(8):
        tiles = []
        for b in range(2):
            three = [blocks[s, 3 * b + t] for t in range(3)]
            last = pltpu.roll(three[0], 32, 1)
            for t in range(1, 3):
                last = jnp.where(group == t, pltpu.roll(three[t], 32 + 32 * t, 1), last)
            tiles += three + [last]
        columns.append(jnp.concatenate(tiles, axis=0).astype(BF16))
    wide = dot(jnp.concatenate(columns, axis=1), yb_ref[...])
    copies = []
    for slot in range(3):
        both = []
        for d in range(8):
            rows = wide[d * 72 + slot * KS : d * 72 + slot * KS + KS]
            both.append(jnp.concatenate([rows[:, :128], rows[:, 128:]], axis=0))
        both = jnp.concatenate(both, axis=1).astype(BF16)
        out = dot(xl_ref[...], jnp.concatenate([both, both], axis=0))
        for d in range(8):
            sent[slot, :, d] = out[:, d * 128 : d * 128 + 128].reshape(16, 8, 128)
        copies.append(pltpu.make_async_copy(sent.at[slot], sent_hbm.at[:, :, slot], sems.at[slot]))
        copies[-1].start()
    for copy in copies:
        copy.wait()


def backward(parts, yb, k):
    return pl.pallas_call(
        backward_kernel,
        out_shape=pltpu.HBM(SENT_SHAPE, F32),
        out_specs=ANY,
        scratch_shapes=[
            pltpu.VMEM((8, *TILES), F32),
            pltpu.VMEM((3, 16, 8, 8, 128), F32),
            pltpu.SemaphoreType.DMA((3,)),
        ],
        compiler_params=params(16),
        cost_estimate=cost(10**9, 4 * 10**6),
        name="backward",
    )(*parts, k["xl_t"], yb)


def spectral_grad_kernel(grads_ref, *refs):
    fields, (spread_ref, wide_ref, out_ref) = refs[:4], refs[4:]
    ky = pl.program_id(0)

    def tile(t):
        value = fields[0][t] + fields[1][t] + fields[2][t] + fields[3][t]
        return value.astype(BF16)

    copies = dot(grads_ref[...].reshape(576, 128).astype(BF16), spread_ref[ky])
    for q in range(4):
        j, t = (ky, q) if q < 3 else (3, ky)
        field = jnp.concatenate([tile(t), tile(3 + t)], axis=0)
        wide = dot(field, wide_ref[j])
        for slot in range(3):
            total = None
            for b in range(2):
                at = b * 72 + slot * KS
                source = (4 * b + q) * 72 + slot * KS
                copy = copies[source : source + KS]
                term = wide[at : at + KS] * jnp.concatenate([copy] * 8, axis=1)
                total = term if total is None else total + term
            out_ref[0, slot * 4 + q] = total


def spectral_grad(grads, fields, k):
    return pl.pallas_call(
        spectral_grad_kernel,
        grid=(3,),
        in_specs=[whole((8, 72, 128))]
        + [whole(TILES)] * 4
        + [whole((4, 128, 128)), whole((4, 128, C * C))],
        out_specs=pl.BlockSpec((1, 12, KS, C * C), lambda i: (i, 0, 0, 0)),
        out_shape=pltpu.HBM((3, 12, KS, C * C), F32),
        compiler_params=params(24),
        cost_estimate=cost(10**9, 4 * 10**6),
        name="spectral_grad",
    )(grads, *fields, *in_hbm(k["spread"], k["wide"]))


def synthesise_kernel(got_ref, table_ref, zl_ref, mixed_hbm, out_hbm, mixed, out, parts, in_sems, out_sems):
    def incoming(n):
        return pltpu.make_async_copy(mixed_hbm.at[n // 4, :, pl.ds(2 * (n % 4), 2)], mixed.at[n], in_sems.at[n])

    def outgoing(n):
        return pltpu.make_async_copy(out.at[n], out_hbm.at[n // 4, :, pl.ds(2 * (n % 4), 2)], out_sems.at[n])

    for n in range(8):
        incoming(n).start()

    def gather(b):
        group = lane_group(8 * KS)
        for half in range(2):
            turned = []
            for q in range(4):
                tiles = []
                for kz in range(KS):
                    block, slot = divmod(2 * kz + half, 3)
                    tiles.append(got_ref[block, 4 * b + q, slot])
                value = jnp.concatenate(tiles, axis=0)
                turned.append(pltpu.roll(value, q * C, 1) if q else value)
            for p in range(4):
                value = turned[(-p) % 4]
                for g in range(1, 4):
                    value = jnp.where(group == g, turned[(g - p) % 4], value)
                value = pltpu.roll(value, 128 - p * C, 1) if p else value
                parts[p, :, half * 128 : half * 128 + 128] = value.astype(BF16)

    def chunk(n, carry):
        @pl.when(n % 4 == 0)
        def _():
            gather(n // 4)

        incoming(n).wait()
        timed = dot(parts[n % 4], table_ref[...]).astype(BF16)
        value = dot(zl_ref[...], timed).reshape(4, 2, N, NT * C)
        out[n] = (value + mixed[n].astype(F32)).astype(BF16)
        outgoing(n).start()
        return carry

    lax.fori_loop(0, 8, chunk, 0)
    for n in range(8):
        outgoing(n).wait()


def synthesise(got, mixed, k):
    vmem = pl.BlockSpec(memory_space=pltpu.VMEM)
    return pl.pallas_call(
        synthesise_kernel,
        in_specs=[vmem, vmem, vmem, ANY],
        out_specs=ANY,
        out_shape=pltpu.HBM(mixed.shape, BF16),
        scratch_shapes=[
            pltpu.VMEM((8, 4, 2, N, NT * C), BF16),
            pltpu.VMEM((8, 4, 2, N, NT * C), BF16),
            pltpu.VMEM((4, 8 * KS, MT * C), BF16),
            pltpu.SemaphoreType.DMA((8,)),
            pltpu.SemaphoreType.DMA((8,)),
        ],
        compiler_params=params(24),
        cost_estimate=cost(4 * 10**9, 10 * 10**6),
        name="synthesise",
    )(got, k["table_t"], k["zl_t"], *in_hbm(mixed))


def exchange_all(block):
    flat = block.reshape(128, 24, 128)
    return lax.all_to_all(flat, ("gx", "gy"), 0, 0, tiled=True).reshape(block.shape)


def exchange_first(block):
    flat = block.reshape(16, 192, 128)
    return lax.all_to_all(flat, "gx", 0, 0, tiled=True).reshape(block.shape)


def body(inputs, cotangent, pre_activation, pointwise, spectral):
    k = constants()
    weights = jnp.transpose(spectral, (1, 2, 0, 3))
    sent = analyse_grad(cotangent, pre_activation, k)
    got = exchange_all(sent)
    sent_input, mix = analyse_input(inputs, pointwise, k)
    mixed = mix_channels(cotangent, pre_activation, mix)
    got, *_ = lax.optimization_barrier((got, sent_input, mixed))
    blocks = planes(got, k)
    sent_input, *_ = lax.optimization_barrier((sent_input, blocks[0]))
    got_input = exchange_first(sent_input)
    modes, grads, yb = mode_grad(exchange_second(blocks), weights, k)
    got_input, *_ = lax.optimization_barrier((got_input, modes))
    sums = reduce_cores(forward(got_input, k))
    back = exchange_first(backward(gather_second(modes), yb, k))
    weight_grad = spectral_grad(grads, reduce_chips(sums), k)
    back, *_ = lax.optimization_barrier((back, weight_grad))
    return synthesise(back, mixed, k), jnp.transpose(weight_grad, (2, 0, 1, 3))


def solution(mesh):
    in_specs = (
        P(None, "gx", "gy", None, None),
        P(None, "gx", "gy", None, None),
        P(None, "gx", "gy", None, None),
        P(),
        P(None, "gy", "gx", None),
    )
    out_specs = (P(None, "gx", "gy", None, None), P(None, "gy", "gx", None))
    return jax.shard_map(body, mesh=mesh, in_specs=in_specs, out_specs=out_specs, check_vma=False)
```

```python
import functools
import math

import jax
import jax.numpy as jnp
import ml_dtypes
import numpy as np
from jax import lax
from jax.experimental import pallas as pl
from jax.experimental.pallas import tpu as pltpu
from jax.sharding import PartitionSpec as P

N = 64
NT = 16
MS = 12
MT = 8
KS = 24
C = 32
BF = ml_dtypes.bfloat16
F32 = jnp.float32
BF16 = jnp.bfloat16
MIB = 1 << 20


def fourier(length, frequencies):
    points = np.arange(length, dtype=np.float64)[:, None]
    orders = np.arange(frequencies, dtype=np.float64)[None, :]
    scales = np.where(orders == 0.0, math.sqrt(1.0 / length), math.sqrt(2.0 / length))
    cosines = scales * np.cos(2.0 * math.pi * points * orders / length)
    sines = math.sqrt(2.0 / length) * np.sin(2.0 * math.pi * points * (orders + 1.0) / length)
    return np.concatenate([cosines, sines], axis=1).astype(np.float32)


def cosine(length, modes):
    points = np.arange(length, dtype=np.float64)[:, None]
    orders = np.arange(modes, dtype=np.float64)[None, :]
    scales = np.where(orders == 0.0, math.sqrt(1.0 / length), math.sqrt(2.0 / length))
    return (scales * np.cos(math.pi * orders * (points + 0.5) / length)).astype(np.float32)


def constants():
    basis = fourier(N, MS)
    third = basis.astype(BF).astype(np.float32)
    time = cosine(NT, MT).astype(BF).astype(np.float32)
    eye_c = np.eye(C, dtype=np.float32)
    eye_r = np.eye(8, dtype=np.float32)
    out = {}
    table = np.einsum("tm,cd->tcmd", time, eye_c).reshape(NT * C, MT * C)
    out["table"] = table.astype(BF)
    out["table_t"] = table.T.copy().astype(BF)
    zl = np.einsum("zk,rs->krsz", third, eye_r).reshape(KS * 8, 8 * N)
    out["zl"] = zl.astype(BF)
    out["zl_t"] = zl.T.copy().astype(BF)
    high = basis.astype(BF).astype(np.float32)
    low = (basis - high).astype(BF).astype(np.float32)
    eye_h = np.eye(2, dtype=np.float32)
    forms = [np.einsum("xk,hg->hkxg", part, eye_h).reshape(2 * KS, 2 * N) for part in (high, low)]
    out["xl"] = np.concatenate(forms, axis=1).astype(BF)
    out["xl_t"] = np.concatenate([form.T for form in forms], axis=1).astype(BF)
    padded = np.zeros((N, 8, 4), np.float32)
    padded[:, :, :3] = basis.reshape(N, 8, 3)
    yb = np.einsum("slhdk,ce->shlcdke", padded.reshape(8, 4, 2, 8, 4), eye_c)
    yb = yb.reshape(8, 256, 1024).astype(BF)
    out["yb"] = yb
    out["yb_t"] = np.swapaxes(yb, 1, 2).copy()
    second = basis.reshape(8, 4, 2, 8, 3)
    out["cy"] = np.repeat(np.einsum("slhdj->djhsl", second).reshape(8, 3, 16, 4), C, axis=3)
    spread = np.zeros((4, 4, C, 4, C), np.float32)
    gather = np.zeros((4, C, C, 4, C), np.float32)
    wide = np.zeros((4, 4, C, C, C), np.float32)
    for j in range(4):
        spread[j, j] = eye_c[:, None, :]
        gather[j, :, :, j, :] = eye_c[:, None, :]
        wide[j, j] = eye_c[:, :, None]
    out["spread"] = spread.reshape(4, 128, 128).astype(BF)
    out["gather"] = gather.reshape(4, C * C, 128).astype(BF)
    out["wide"] = wide.reshape(4, 128, C * C).astype(BF)
    return out


def dot(a, b):
    return jnp.dot(a, b, preferred_element_type=F32)


def dot_t(a, b):
    return lax.dot_general(a, b, (((1,), (1,)), ((), ())), preferred_element_type=F32)


def gelu_slope(v):
    cdf = 0.5 * (1.0 + lax.erf(v * 0.7071067811865476))
    return cdf + v * (0.3989422804014327 * jnp.exp(-0.5 * v * v))


def lane_group(rows):
    return lax.broadcasted_iota(jnp.int32, (rows, 128), 1) // C


def send_parts(parts, sent_ref):
    group = lane_group(8 * KS)
    for half in range(2):
        lanes = slice(half * 128, half * 128 + 128)
        turned = [parts[p, :, lanes] for p in range(4)]
        turned = [pltpu.roll(value, p * C, 1) if p else value for p, value in enumerate(turned)]
        for q in range(4):
            value = turned[(-q) % 4]
            for p in range(1, 4):
                value = jnp.where(group == p, turned[(p - q) % 4], value)
            if q:
                value = pltpu.roll(value, 128 - q * C, 1)
            for kz in range(KS):
                block, slot = divmod(2 * kz + half, 3)
                sent_ref[block, q, slot] = value[kz * 8 : kz * 8 + 8]


def analyse_grad_kernel(cot_ref, pre_ref, table_ref, zl_ref, sent_ref, even, odd, parts):
    step = pl.program_id(1)

    def cells(pair, flat):
        for x in range(4):
            for y in range(2):
                for j in range(4):
                    rows = slice(j * 16, j * 16 + 16)
                    v = pre_ref[0, x, 2 * pair + y, rows, :].astype(F32)
                    g = cot_ref[0, x, 2 * pair + y, rows, :].astype(F32)
                    at = (2 * x + y) * N + j * 16
                    flat[at : at + 16, :] = (g * gelu_slope(v)).astype(BF16)

    def analyse(pair, flat):
        sectioned = dot(zl_ref[...], flat[...]).astype(BF16)
        parts[pair] = dot(sectioned, table_ref[...])

    analyse((2 * step + 3) % 4, odd)
    cells(0, even)
    analyse(2 * step, even)
    cells(1, odd)

    @pl.when(step == 1)
    def _():
        analyse(3, odd)
        send_parts(parts, sent_ref)


def analyse_input_kernel(field_ref, table_ref, zl_ref, weight_ref, sent_ref, mix_ref, parts):
    step = pl.program_id(1)

    @pl.when((step == 0) & (pl.program_id(0) == 0))
    def _():
        rows = lax.broadcasted_iota(jnp.int32, (256, C), 0) % C
        copies = (rows == lax.broadcasted_iota(jnp.int32, (256, C), 1)).astype(BF16)
        mixed = dot_t(dot_t(copies, weight_ref[...]).astype(BF16), copies)
        blocks = [lax.broadcasted_iota(jnp.int32, (256, 256), axis) // C for axis in range(2)]
        mix_ref[...] = jnp.where(blocks[0] == blocks[1], mixed, 0.0).astype(BF16)
    for pair in range(2):
        field = field_ref[0, :, 2 * pair : 2 * pair + 2].reshape(8 * N, NT * C)
        sectioned = dot(zl_ref[...], field).astype(BF16)
        parts[2 * step + pair] = dot(sectioned, table_ref[...])

    @pl.when(step == 1)
    def _():
        send_parts(parts, sent_ref)


FIELD = pl.BlockSpec((1, 4, 4, N, NT * C), lambda b, p: (b, 0, p, 0, 0))
SENT = pl.BlockSpec((16, 4, 3, 8, 128), lambda b, p: (0, b, 0, 0, 0))
SENT_SHAPE = (16, 8, 3, 8, 128)
TILES = (6, 72, 128)
ANY = pl.BlockSpec(memory_space=pl.ANY)


def whole(shape):
    return pl.BlockSpec(shape, lambda *ids: (0,) * len(shape))


def params(limit):
    return pltpu.CompilerParams(vmem_limit_bytes=limit * MIB)


def cost(flops, nbytes):
    return pl.CostEstimate(flops=flops, bytes_accessed=nbytes, transcendentals=0)


def in_hbm(*arrays):
    return [pltpu.with_memory_space_constraint(a, pltpu.HBM) for a in arrays]


def analyse_grad(cotangent, pre_activation, k):
    return pl.pallas_call(
        analyse_grad_kernel,
        grid=(2, 2),
        in_specs=[FIELD, FIELD, whole((NT * C, MT * C)), whole((8 * KS, 8 * N))],
        out_specs=SENT,
        out_shape=pltpu.HBM(SENT_SHAPE, F32),
        scratch_shapes=[
            pltpu.VMEM((8 * N, NT * C), BF16),
            pltpu.VMEM((8 * N, NT * C), BF16),
            pltpu.VMEM((4, 8 * KS, MT * C), F32),
        ],
        compiler_params=params(24),
        cost_estimate=cost(4 * 10**9, 14 * 10**6),
        name="analyse_grad",
    )(*in_hbm(cotangent, pre_activation, k["table"], k["zl"]))


def mix_channels_kernel(cot_ref, pre_ref, mix_ref, out_ref, even, odd):
    def cells(pair, flat):
        for x in range(4):
            for y in range(2):
                for j in range(4):
                    rows = slice(j * 16, j * 16 + 16)
                    v = pre_ref[0, x, 2 * pair + y, rows, :].astype(F32)
                    g = cot_ref[0, x, 2 * pair + y, rows, :].astype(F32)
                    at = (2 * x + y) * N + j * 16
                    flat[at : at + 16, :] = (g * gelu_slope(v)).astype(BF16)

    def mix(pair, flat):
        for side in range(2):
            lanes = slice(side * 256, side * 256 + 256)
            mixed = dot(flat[:, lanes], mix_ref[...]).astype(BF16)
            out_ref[0, :, 2 * pair : 2 * pair + 2, :, lanes] = mixed.reshape(4, 2, N, 256)

    cells(0, even)
    mix(0, even)
    cells(1, odd)
    mix(1, odd)


def mix_channels(cotangent, pre_activation, mix):
    return pl.pallas_call(
        mix_channels_kernel,
        grid=(2, 2),
        in_specs=[FIELD, FIELD, whole((256, 256))],
        out_specs=FIELD,
        out_shape=pltpu.HBM(cotangent.shape, BF16),
        scratch_shapes=[pltpu.VMEM((8 * N, NT * C), BF16)] * 2,
        compiler_params=params(24),
        cost_estimate=cost(4 * 10**9, 12 * 10**6),
        name="mix_channels",
    )(*in_hbm(cotangent, pre_activation, mix))


def analyse_input(inputs, pointwise, k):
    return pl.pallas_call(
        analyse_input_kernel,
        grid=(2, 2),
        in_specs=[FIELD, whole((NT * C, MT * C)), whole((8 * KS, 8 * N)), whole((C, C))],
        out_specs=[SENT, whole((256, 256))],
        out_shape=[pltpu.HBM(SENT_SHAPE, F32), pltpu.HBM((256, 256), BF16)],
        scratch_shapes=[pltpu.VMEM((4, 8 * KS, MT * C), F32)],
        compiler_params=params(24),
        cost_estimate=cost(4 * 10**9, 6 * 10**6),
        name="analyse_input",
    )(*in_hbm(inputs, k["table"], k["zl"], pointwise))


def mode_of(j, t):
    return (j, t) if j < 3 else (t, 3)


def forward_kernel(got_ref, xl_ref, yb_hbm, keep_ref, cross_ref, yb_ref, fields, blocks, sem):
    me = lax.axis_index("gy")
    copy = pltpu.make_async_copy(yb_hbm.at[me], yb_ref, sem)
    copy.start()
    for slot in range(3):
        field = jnp.concatenate(
            [got_ref[:, d, slot].reshape(128, 128).astype(BF16) for d in range(8)], axis=1
        )
        wide = dot(xl_ref[...], jnp.concatenate([field, field], axis=0))
        for d in range(8):
            for half in range(2):
                rows = slice(d * 72 + slot * KS, d * 72 + slot * KS + KS)
                fields[rows, half * 128 : half * 128 + 128] = wide[
                    half * KS : half * KS + KS, d * 128 : d * 128 + 128
                ]
    copy.wait()
    group = lane_group(72)
    field = fields[...].astype(BF16)
    for to in range(8):
        part = dot(field, yb_ref[:, to * 128 : to * 128 + 128])
        for b in range(2):
            last = part[(4 * b + 3) * 72 : (4 * b + 4) * 72]
            for t in range(3):
                value = part[(4 * b + t) * 72 : (4 * b + t + 1) * 72]
                blocks[to, 3 * b + t] = jnp.where(group == 3, pltpu.roll(last, 96 - 32 * t, 1), value)
    for sx in range(4):
        keep_ref[sx] = blocks[me ^ (2 * sx)]
        cross_ref[sx] = blocks[me ^ (2 * sx + 1)]


def forward(got, k):
    vmem = pl.BlockSpec(memory_space=pltpu.VMEM)
    return pl.pallas_call(
        forward_kernel,
        in_specs=[vmem, vmem, ANY],
        out_shape=[jax.ShapeDtypeStruct((4, *TILES), F32)] * 2,
        scratch_shapes=[
            pltpu.VMEM((256, 1024), BF16),
            pltpu.VMEM((576, 256), F32),
            pltpu.VMEM((8, *TILES), F32),
            pltpu.SemaphoreType.DMA,
        ],
        compiler_params=params(16),
        cost_estimate=cost(10**9, 4 * 10**6),
        name="forward",
    )(got, k["xl"], *in_hbm(k["yb"]))


def add_cores_kernel(keep_ref, cross_ref, *outs):
    for sx in range(4):
        outs[sx][...] = keep_ref[sx] + cross_ref[sx]


def add_cores(keep, cross):
    return pl.pallas_call(
        add_cores_kernel,
        out_shape=[jax.ShapeDtypeStruct(TILES, F32)] * 4,
        compiler_params=params(16),
        cost_estimate=cost(10**6, 10**6),
        name="add_cores",
    )(keep, cross)


def across(block, sx):
    return lax.ppermute(block, "gy", [(i, i ^ sx) for i in range(8)])


def reduce_cores(blocks):
    keep, cross = blocks
    return add_cores(keep, across(cross, 1))


def reduce_chips(sums):
    own, *others = sums
    return [own] + [across(other, 2 * sx + 2) for sx, other in enumerate(others)]


def gather_second(block):
    parts = [block, across(block, 1)]
    for sx in range(1, 4):
        far = across(block, 2 * sx)
        parts += [far, across(far, 1)]
    return parts


def transform_x(got_ref, xl_ref, planes):
    for slot in range(3):
        field = jnp.concatenate(
            [got_ref[:, s, slot].reshape(128, 128).astype(BF16) for s in range(8)], axis=1
        )
        wide = dot(xl_ref[...], jnp.concatenate([field, field], axis=0))
        for s in range(8):
            planes[s, slot * 48 : slot * 48 + 48, :] = wide[:, s * 128 : s * 128 + 128]


def transform_y(planes, cy_ref, blocks):
    group = lane_group(72)

    def block(d, carry):
        totals = [jnp.zeros((72, 128), F32)] * 3
        for s in range(8):
            for half in range(2):
                starts = [slot * 48 + half * KS for slot in range(3)]
                rows = jnp.concatenate([planes[s, at : at + KS, :] for at in starts], axis=0)
                for j in range(3):
                    totals[j] = totals[j] + rows * cy_ref[d, j, half * 8 + s : half * 8 + s + 1, :]
        value = jnp.zeros((72, 128), F32)
        for j in range(3):
            total = totals[j] + pltpu.roll(totals[j], 64, 1)
            total = total + pltpu.roll(total, 32, 1)
            value = jnp.where(group == j, total, value)
        blocks[d] = value
        return carry

    lax.fori_loop(0, 8, block, 0)


def group_shape(rows):
    return jax.ShapeDtypeStruct((4, rows, 128), F32)


def deal(blocks, keep_ref, cross_ref):
    me = lax.axis_index("gy")
    for sx in range(4):
        keep_ref[sx] = blocks[me ^ (2 * sx)]
        cross_ref[sx] = blocks[me ^ (2 * sx + 1)]


def arrived(refs):
    keep, cross, *far = refs
    return [keep.at[0], cross.at[0]] + [ref.at[i] for ref in far for i in range(2)]


def collect(parts, blocks):
    me = lax.axis_index("gy")
    for s in range(8):
        blocks[me ^ s] = parts[s][...]


def planes_kernel(got_ref, xl_ref, cy_hbm, keep_ref, cross_ref, cy_ref, planes, blocks, sem):
    copy = pltpu.make_async_copy(cy_hbm, cy_ref, sem)
    copy.start()
    transform_x(got_ref, xl_ref, planes)
    copy.wait()
    transform_y(planes, cy_ref, blocks)
    deal(blocks, keep_ref, cross_ref)


def planes(got, k):
    vmem = pl.BlockSpec(memory_space=pltpu.VMEM)
    return pl.pallas_call(
        planes_kernel,
        in_specs=[vmem, vmem, ANY],
        out_shape=[group_shape(72)] * 2,
        scratch_shapes=[
            pltpu.VMEM((8, 3, 16, 128), F32),
            pltpu.VMEM((8, 144, 128), F32),
            pltpu.VMEM((8, 72, 128), F32),
            pltpu.SemaphoreType.DMA,
        ],
        compiler_params=params(16),
        cost_estimate=cost(10**9, 3 * 10**6),
        name="planes",
    )(got, k["xl"], *in_hbm(k["cy"]))


def pair_up_kernel(keep_ref, cross_ref, *outs):
    for sx in range(1, 4):
        outs[sx - 1][0] = keep_ref[sx]
        outs[sx - 1][1] = cross_ref[sx]


def pair_up(keep, cross):
    shape = jax.ShapeDtypeStruct((2, *keep.shape[1:]), F32)
    return pl.pallas_call(
        pair_up_kernel,
        out_shape=[shape] * 3,
        compiler_params=params(16),
        cost_estimate=cost(10**6, 10**6),
        name="pair_up",
    )(keep, cross)


def exchange_cores(blocks):
    keep, cross = blocks
    cross = across(cross, 1)
    return keep, cross, pair_up(keep, cross)


def exchange_chips(keep, cross, pairs):
    return [keep, cross] + [across(pair, 2 * sx + 2) for sx, pair in enumerate(pairs)]


def mode_grad_kernel(*refs):
    parts, (spread_ref, weight_hbm, gather_hbm, yb_hbm) = arrived(refs[:5]), refs[5:9]
    out_ref, grads_ref, yb_ref, weight_ref, gather_ref, sems = refs[9:]
    copies = []
    for ky in range(3):
        copies.append(pltpu.make_async_copy(weight_hbm.at[ky], weight_ref.at[ky], sems.at[0, ky]))
        copies.append(pltpu.make_async_copy(gather_hbm.at[ky], gather_ref.at[ky], sems.at[1, ky]))
    copies.append(pltpu.make_async_copy(yb_hbm.at[lax.axis_index("gy")], yb_ref, sems.at[0, 3]))
    for copy in copies:
        copy.start()
    collect(parts, grads_ref)
    field = []
    for b in range(2):
        for slot in range(3):
            for q in range(4):
                field.append(grads_ref[4 * b + q, slot * KS : slot * KS + KS, :])
    field = jnp.concatenate(field, axis=0).astype(BF16)
    total = None
    for ky in range(3):
        lanes = dot(field, spread_ref[ky]).astype(BF16)
        copies[2 * ky].wait()
        products = []
        for b in range(2):
            copy = lanes[b * 288 : b * 288 + 288]
            products.append(weight_ref[ky] * jnp.concatenate([copy] * 8, axis=1))
        copies[2 * ky + 1].wait()
        term = dot(jnp.concatenate(products, axis=0), gather_ref[ky])
        total = term if total is None else total + term
    group = lane_group(72)
    for b in range(2):
        modes = []
        for q in range(4):
            starts = [b * 288 + (slot * 4 + q) * KS for slot in range(3)]
            modes.append(jnp.concatenate([total[at : at + KS] for at in starts], axis=0))
        for t in range(3):
            out_ref[3 * b + t] = jnp.where(group == 3, pltpu.roll(modes[3], 96 - 32 * t, 1), modes[t])
    copies[6].wait()


def mode_grad(parts, weights, k):
    vmem = pl.BlockSpec(memory_space=pltpu.VMEM)
    return pl.pallas_call(
        mode_grad_kernel,
        in_specs=[vmem] * 6 + [ANY] * 3,
        out_shape=[
            jax.ShapeDtypeStruct(TILES, F32),
            jax.ShapeDtypeStruct((8, 72, 128), F32),
            pltpu.VMEM((1024, 256), BF16),
        ],
        scratch_shapes=[
            pltpu.VMEM((3, 12 * KS, C * C), BF16),
            pltpu.VMEM((4, C * C, 128), BF16),
            pltpu.SemaphoreType.DMA((2, 4)),
        ],
        compiler_params=params(16),
        cost_estimate=cost(10**9, 4 * 10**6),
        name="mode_grad",
    )(*parts, k["spread"], *in_hbm(weights.reshape(3, 12 * KS, C * C), k["gather"], k["yb_t"]))


def backward_kernel(*refs):
    parts, (xl_ref, yb_ref, sent_hbm, blocks, sent, sems) = refs[:8], refs[8:]
    me = lax.axis_index("gy")
    for s in range(8):
        blocks[me ^ s] = parts[s][...]
    group = lane_group(72)
    columns = []
    for s in range(8):
        tiles = []
        for b in range(2):
            three = [blocks[s, 3 * b + t] for t in range(3)]
            last = pltpu.roll(three[0], 32, 1)
            for t in range(1, 3):
                last = jnp.where(group == t, pltpu.roll(three[t], 32 + 32 * t, 1), last)
            tiles += three + [last]
        columns.append(jnp.concatenate(tiles, axis=0).astype(BF16))
    wide = dot(jnp.concatenate(columns, axis=1), yb_ref[...])
    copies = []
    for slot in range(3):
        both = []
        for d in range(8):
            rows = wide[d * 72 + slot * KS : d * 72 + slot * KS + KS]
            both.append(jnp.concatenate([rows[:, :128], rows[:, 128:]], axis=0))
        both = jnp.concatenate(both, axis=1).astype(BF16)
        out = dot(xl_ref[...], jnp.concatenate([both, both], axis=0))
        for d in range(8):
            sent[slot, :, d] = out[:, d * 128 : d * 128 + 128].reshape(16, 8, 128)
        copies.append(pltpu.make_async_copy(sent.at[slot], sent_hbm.at[:, :, slot], sems.at[slot]))
        copies[-1].start()
    for copy in copies:
        copy.wait()


def backward(parts, yb, k):
    return pl.pallas_call(
        backward_kernel,
        out_shape=pltpu.HBM(SENT_SHAPE, F32),
        out_specs=ANY,
        scratch_shapes=[
            pltpu.VMEM((8, *TILES), F32),
            pltpu.VMEM((3, 16, 8, 8, 128), F32),
            pltpu.SemaphoreType.DMA((3,)),
        ],
        compiler_params=params(16),
        cost_estimate=cost(10**9, 4 * 10**6),
        name="backward",
    )(*parts, k["xl_t"], yb)


def spectral_grad_kernel(grads_ref, *refs):
    fields, (spread_ref, wide_ref, out_ref) = refs[:4], refs[4:]
    ky = pl.program_id(0)

    def tile(t):
        value = fields[0][t] + fields[1][t] + fields[2][t] + fields[3][t]
        return value.astype(BF16)

    copies = dot(grads_ref[...].reshape(576, 128).astype(BF16), spread_ref[ky])
    for q in range(4):
        j, t = (ky, q) if q < 3 else (3, ky)
        field = jnp.concatenate([tile(t), tile(3 + t)], axis=0)
        wide = dot(field, wide_ref[j])
        for slot in range(3):
            total = None
            for b in range(2):
                at = b * 72 + slot * KS
                source = (4 * b + q) * 72 + slot * KS
                copy = copies[source : source + KS]
                term = wide[at : at + KS] * jnp.concatenate([copy] * 8, axis=1)
                total = term if total is None else total + term
            out_ref[0, slot * 4 + q] = total


def spectral_grad(grads, fields, k):
    return pl.pallas_call(
        spectral_grad_kernel,
        grid=(3,),
        in_specs=[whole((8, 72, 128))]
        + [whole(TILES)] * 4
        + [whole((4, 128, 128)), whole((4, 128, C * C))],
        out_specs=pl.BlockSpec((1, 12, KS, C * C), lambda i: (i, 0, 0, 0)),
        out_shape=pltpu.HBM((3, 12, KS, C * C), F32),
        compiler_params=params(24),
        cost_estimate=cost(10**9, 4 * 10**6),
        name="spectral_grad",
    )(grads, *fields, *in_hbm(k["spread"], k["wide"]))


def synthesise_kernel(got_ref, table_ref, zl_ref, mixed_hbm, out_hbm, mixed, out, parts, in_sems, out_sems):
    def incoming(n):
        return pltpu.make_async_copy(mixed_hbm.at[n // 4, :, pl.ds(2 * (n % 4), 2)], mixed.at[n], in_sems.at[n])

    def outgoing(n):
        return pltpu.make_async_copy(out.at[n], out_hbm.at[n // 4, :, pl.ds(2 * (n % 4), 2)], out_sems.at[n])

    for n in range(8):
        incoming(n).start()

    def gather(b):
        group = lane_group(8 * KS)
        for half in range(2):
            turned = []
            for q in range(4):
                tiles = []
                for kz in range(KS):
                    block, slot = divmod(2 * kz + half, 3)
                    tiles.append(got_ref[block, 4 * b + q, slot])
                value = jnp.concatenate(tiles, axis=0)
                turned.append(pltpu.roll(value, q * C, 1) if q else value)
            for p in range(4):
                value = turned[(-p) % 4]
                for g in range(1, 4):
                    value = jnp.where(group == g, turned[(g - p) % 4], value)
                value = pltpu.roll(value, 128 - p * C, 1) if p else value
                parts[p, :, half * 128 : half * 128 + 128] = value.astype(BF16)

    def chunk(n, carry):
        @pl.when(n % 4 == 0)
        def _():
            gather(n // 4)

        incoming(n).wait()
        timed = dot(parts[n % 4], table_ref[...]).astype(BF16)
        value = dot(zl_ref[...], timed).reshape(4, 2, N, NT * C)
        out[n] = (value + mixed[n].astype(F32)).astype(BF16)
        outgoing(n).start()
        return carry

    lax.fori_loop(0, 8, chunk, 0)
    for n in range(8):
        outgoing(n).wait()


def synthesise(got, mixed, k):
    vmem = pl.BlockSpec(memory_space=pltpu.VMEM)
    return pl.pallas_call(
        synthesise_kernel,
        in_specs=[vmem, vmem, vmem, ANY],
        out_specs=ANY,
        out_shape=pltpu.HBM(mixed.shape, BF16),
        scratch_shapes=[
            pltpu.VMEM((8, 4, 2, N, NT * C), BF16),
            pltpu.VMEM((8, 4, 2, N, NT * C), BF16),
            pltpu.VMEM((4, 8 * KS, MT * C), BF16),
            pltpu.SemaphoreType.DMA((8,)),
            pltpu.SemaphoreType.DMA((8,)),
        ],
        compiler_params=params(24),
        cost_estimate=cost(4 * 10**9, 10 * 10**6),
        name="synthesise",
    )(got, k["table_t"], k["zl_t"], *in_hbm(mixed))


def exchange_all(block):
    flat = block.reshape(128, 24, 128)
    return lax.all_to_all(flat, ("gx", "gy"), 0, 0, tiled=True).reshape(block.shape)


def exchange_first(block):
    flat = block.reshape(16, 192, 128)
    return lax.all_to_all(flat, "gx", 0, 0, tiled=True).reshape(block.shape)


def body(inputs, cotangent, pre_activation, pointwise, spectral):
    k = constants()
    weights = jnp.transpose(spectral, (1, 2, 0, 3))
    sent = analyse_grad(cotangent, pre_activation, k)
    got = exchange_all(sent)
    sent_input, mix = analyse_input(inputs, pointwise, k)
    mixed = mix_channels(cotangent, pre_activation, mix)
    got, *_ = lax.optimization_barrier((got, sent_input, mixed))
    blocks = planes(got, k)
    keep, cross, pairs = exchange_cores(blocks)
    sent_input, *_ = lax.optimization_barrier((sent_input, pairs[0]))
    got_input = exchange_first(sent_input)
    modes, grads, yb = mode_grad(exchange_chips(keep, cross, pairs), weights, k)
    got_input, *_ = lax.optimization_barrier((got_input, modes))
    sums = reduce_cores(forward(got_input, k))
    back = exchange_first(backward(gather_second(modes), yb, k))
    weight_grad = spectral_grad(grads, reduce_chips(sums), k)
    back, *_ = lax.optimization_barrier((back, weight_grad))
    return synthesise(back, mixed, k), jnp.transpose(weight_grad, (2, 0, 1, 3))


def solution(mesh):
    in_specs = (
        P(None, "gx", "gy", None, None),
        P(None, "gx", "gy", None, None),
        P(None, "gx", "gy", None, None),
        P(),
        P(None, "gy", "gx", None),
    )
    out_specs = (P(None, "gx", "gy", None, None), P(None, "gy", "gx", None))
    return jax.shard_map(body, mesh=mesh, in_specs=in_specs, out_specs=out_specs, check_vma=False)
```
